256 devices in a mesh: fx: 8 (over z), fy: 16 (over x, y), grp: 2 (over core).
Axes of the slice: x: 4, y: 4, z: 8, core: 2. Of those that a mesh axis runs over, the one named last changes fastest.
Arguments:
- efield: float32 [3, 32, 128, 4096], P(None, None, 'fx', ('fy', 'grp')), may hold values from -6 to 6
- hfield: float32 [3, 32, 128, 4096], P(None, None, 'fx', ('fy', 'grp')), may hold values from -6 to 6
- loss_coef: float32 [32, 128, 4096], P(None, 'fx', ('fy', 'grp')), may hold values from 0.8 to 1
- update_coef: float32 [32, 128, 4096], P(None, 'fx', ('fy', 'grp')), may hold values from 0.2 to 0.6
- port_count: int32 [256], replicated, may hold values from 1 to 32, 4096 in all
- port_perm: int32 [4096], replicated, may hold values from 0 to 4095, each once
- port_cell: int32 [256, 32], P(('fx', 'fy', 'grp')), may hold values from 0 to 2047
- pole_state: float32 [2048, 256], P(('fx', 'fy', 'grp')), may hold values from -6 to 6
- transition: float32 [2048, 256, 256], P(('fx', 'fy', 'grp')), may hold values from -0.25 to 0.25
- input_map: float32 [2048, 256, 2], P(('fx', 'fy', 'grp')), may hold values from -6 to 6
- output_map: float32 [2048, 2, 256], P(('fx', 'fy', 'grp')), may hold values from -0.375 to 0.375
- feedthrough: float32 [2048, 2, 2], P(('fx', 'fy', 'grp')), may hold values from -4 to 4
Outputs:
- efield_out: float32 [3, 32, 128, 4096], P(None, None, 'fx', ('fy', 'grp'))
- hfield_out: float32 [3, 32, 128, 4096], P(None, None, 'fx', ('fy', 'grp'))
- final_state: float32 [2048, 256], P(('fx', 'fy', 'grp'))
The draws below stay inside these ranges and needn't reach their ends.
Inputs may be any that keep to these rules, and one draw needn't show every extreme that they name: `port_count`: each tile holds between 1 and 32 ports, 4096 in all; some tile holds exactly 32. `port_perm`: each live port number once. `port_cell`: cell x * 128 + y within the tile; slots at or beyond the tile's port_count are unused.
All inputs are finite; a program needn't handle non-finite values.
Results may differ from the reference program's by a relative error of at most 0.0003.
Values sent between devices are 32-bit elements; how exact they have to be, the bound alone decides.
No kernel may reach another device: no remote copies, remote signals or barrier semaphores. Data moves between devices by JAX's collectives and lax.ppermute only.
A program may use at most 64 MiB of HBM per device.

```python
import math
import jax
import jax.numpy as jnp
import numpy as np
from jax import lax

CX = 16
CY = 128
NZ = 32
K = 4
BLOCKS = 2
P_SIZE = 256
NX = 128
NY = 4096
TILES_Y = 32
TILES = 256
NM = 2048
NPORT = 4096
PMAX = 32


def with_ends(entries, own_key, smallest, largest):
    extent = entries.shape
    index_at = [jax.random.randint(jax.random.fold_in(own_key, axis), (), 0, extent[axis]) for axis in range(len(extent))]
    entries = entries.at[tuple(index_at)].set(smallest)
    longest = extent.index(max(extent))
    index_at[longest] = (index_at[longest] + 1) % extent[longest]
    return entries.at[tuple(index_at)].set(largest)


def shard_levels(stream_key, extent, cuts, least, largest):
    def one(dim, parts):
        draws = jax.random.uniform(jax.random.fold_in(jax.random.fold_in(stream_key, 6), dim), (parts,), jnp.float32, least / len(cuts), largest / len(cuts))
        return jnp.repeat(jnp.exp(draws), extent[dim] // parts).reshape((-1,) + (1,) * (len(extent) - dim - 1))

    level = one(*cuts[0])
    for cut in cuts[1:]:
        level = level * one(*cut)
    return level


def split_up(count, total, limit, lean):
    portions = [(1 << 20) // math.isqrt(rank ** lean) + 1 for rank in range(2, count + 1)]
    spare, given = total - limit - (count - 1), [1] * (count - 1)
    while spare > 0:
        free = [i for i in range(count - 1) if given[i] < limit]
        mass, left = sum([portions[i] for i in free]), spare
        for i in free:
            more = min(limit - given[i], max(1, left * portions[i] // mass), spare)
            given[i] = given[i] + more
            spare = spare - more
    return np.array([limit] + given)


def uneven_parts(own_key, number_of, total, bound, skew):
    if number_of == 2:
        one = jax.random.randint(own_key, (), max(1, total - bound), min(bound, total - 1) + 1)
        return jnp.stack([one, total - one])
    lengths = jnp.asarray(split_up(number_of, total, bound, skew), jnp.int32)
    twos = (number_of - 1) // 2
    source_of, sink = lengths[1:1 + 2 * twos:2], lengths[2:2 + 2 * twos:2]
    room = jnp.minimum(source_of - 1, bound - sink)
    moved = jax.random.randint(jax.random.fold_in(own_key, 1), (twos,), 0, 1 << 20) % (room + 1)
    lengths = lengths.at[1:1 + 2 * twos:2].set(source_of - moved).at[2:2 + 2 * twos:2].set(sink + moved)
    return lengths[jax.random.permutation(jax.random.fold_in(own_key, 2), number_of)]


def normal_values(own_key, shape, scale, bound, split=(), held_as=jnp.bfloat16):
    result = jax.random.normal(own_key, shape, jnp.float32) * scale
    if len(split) > 0:
        result = shard_levels(own_key, shape, split, -0.22, 0.18) * result
    return jnp.clip(result, min=-bound, max=bound).astype(held_as)


def setup_inputs(seed: int = 0) -> dict:
    splits = jax.random.split(jax.random.key(seed), 13)
    return {
        "efield": normal_values(splits[0], (3, NZ, NX, NY), 1.0, 6.0, ((2, 8), (3, 32)), jnp.float32),
        "hfield": normal_values(splits[1], (3, NZ, NX, NY), 1.0, 6.0, ((2, 8), (3, 32)), jnp.float32),
        "loss_coef": jnp.clip(0.8 + 0.19999999 * jax.random.uniform(splits[2], (NZ, NX, NY), jnp.float32) ** shard_levels(splits[2], (NZ, NX, NY), ((1, 8), (2, 32)), -0.2, 0.2), 0.8, 1.0),
        "update_coef": jnp.clip(0.2 + 0.400000021 * jax.random.uniform(splits[3], (NZ, NX, NY), jnp.float32) ** shard_levels(splits[3], (NZ, NX, NY), ((1, 8), (2, 32)), -0.2, 0.2), 0.2, 0.6),
        "port_count": uneven_parts(splits[4], TILES, NPORT, PMAX, 2).astype(jnp.int32),
        "port_perm": jax.random.permutation(splits[5], NPORT).astype(jnp.int32),
        "port_cell": with_ends(jax.random.randint(splits[6], (TILES, PMAX), 0, CX * CY), jax.random.fold_in(splits[6], 1), 0, (CX * CY) - 1).astype(jnp.int32),
        "pole_state": normal_values(splits[7], (NM, P_SIZE), 1.0, 6.0, ((0, 256),), jnp.float32),
        "transition": normal_values(splits[8], (NM, P_SIZE, P_SIZE), (2 * P_SIZE) ** -0.5, 0.25, ((0, 256),), jnp.float32),
        "input_map": normal_values(splits[9], (NM, P_SIZE, 2), 1 ** -0.5, 6.0, ((0, 256),), jnp.float32),
        "output_map": normal_values(splits[10], (NM, 2, P_SIZE), P_SIZE ** -0.5, 0.375, ((0, 256),), jnp.float32),
        "feedthrough": normal_values(splits[11], (NM, 2, 2), 2 ** -0.5, 4.0, ((0, 256),), jnp.float32),
    }


COURANT = 0.5
HIGH = lax.Precision.HIGHEST


def forward(field, axis, after):
    ahead = jnp.concatenate([lax.slice_in_dim(field, 1, field.shape[axis], axis=axis), after], axis=axis)
    return ahead - field


def backward(field, axis, before):
    behind = jnp.concatenate([before, lax.slice_in_dim(field, 0, field.shape[axis] - 1, axis=axis)], axis=axis)
    return field - behind


def edge(field, axis):
    return jnp.zeros_like(lax.slice_in_dim(field, 0, 1, axis=axis))


def update_magnetic(electric, magnetic, next_x, next_y):
    elec_x, elec_y, elec_z = electric
    magn_x, magn_y, magn_z = magnetic
    flat = edge(elec_x, 0)
    magn_x = magn_x - COURANT * (forward(elec_z, 2, next_y[1]) - forward(elec_y, 0, flat))
    magn_y = magn_y - COURANT * (forward(elec_x, 0, flat) - forward(elec_z, 1, next_x[1]))
    magn_z = magn_z - COURANT * (forward(elec_y, 1, next_x[0]) - forward(elec_x, 2, next_y[0]))
    return (magn_x, magn_y, magn_z)


def update_electric(electric, magnetic, loss, gain, source, prev_x, prev_y):
    elec_x, elec_y, elec_z = electric
    magn_x, magn_y, magn_z = magnetic
    flat = edge(magn_x, 0)
    elec_x = loss * elec_x + gain * (backward(magn_z, 2, prev_y[1]) - backward(magn_y, 0, flat))
    elec_y = loss * elec_y + gain * (backward(magn_x, 0, flat) - backward(magn_z, 1, prev_x[1]))
    elec_z = loss * elec_z + gain * (backward(magn_y, 1, prev_x[0]) - backward(magn_x, 2, prev_y[0]) - source)
    return (elec_x, elec_y, elec_z)


def reference(efield, hfield, loss_coef, update_coef, port_count, port_perm, port_cell, pole_state, transition, input_map, output_map, feedthrough):
    starts = (jnp.cumsum(port_count) - port_count).astype(jnp.int32)
    tile = (jnp.sum((starts[None, :] <= port_perm[:, None]).astype(jnp.int32), axis=1) - 1).astype(jnp.int32)
    slot = (port_perm - starts[tile]).astype(jnp.int32)
    cell = port_cell[tile, slot]
    column_x = (tile // TILES_Y) * CX + cell // CY
    column_y = (tile % TILES_Y) * CY + cell % CY
    electric = (efield[0], efield[1], efield[2])
    magnetic = (hfield[0], hfield[1], hfield[2])
    state = pole_state
    for block in range(BLOCKS):
        voltage = jnp.mean(electric[2][:, column_x, column_y], axis=0).reshape(NM, 2)
        current = jnp.einsum("mqp,mp->mq", output_map, state, precision=HIGH) + jnp.einsum("mqr,mr->mq", feedthrough, voltage, precision=HIGH)
        state = jnp.einsum("mpr,mr->mp", transition, state, precision=HIGH) + jnp.einsum("mpq,mq->mp", input_map, voltage, precision=HIGH)
        source = jnp.zeros((NX, NY), jnp.float32).at[column_x, column_y].add(current.reshape(-1))
        for step in range(K):
            next_x = (edge(electric[1], 1), edge(electric[2], 1))
            next_y = (edge(electric[0], 2), edge(electric[2], 2))
            magnetic = update_magnetic(electric, magnetic, next_x, next_y)
            prev_x = (edge(magnetic[1], 1), edge(magnetic[2], 1))
            prev_y = (edge(magnetic[0], 2), edge(magnetic[2], 2))
            electric = update_electric(electric, magnetic, loss_coef, update_coef, source, prev_x, prev_y)
    return jnp.stack(electric), jnp.stack(magnetic), state
```

```python
import functools

import jax
import jax.numpy as jnp
from jax import lax
from jax.experimental import pallas as pl
from jax.experimental.pallas import tpu as pltpu
from jax.sharding import PartitionSpec as P

K = 4
BLOCKS = 2
COURANT = 0.5
HIGH = lax.Precision.HIGHEST
ALL = ("fx", "fy", "grp")
Z, X, Y = 32, 16, 128
SLOTS = 32
LIST = 9 * SLOTS
MODELS = 8
F32 = jnp.float32
I32 = jnp.int32
LANE_O, LANE_D, LANE_C = 32, 48, 80
OWN, MATE, DRAWN, SELF, CROSS, CELL, MASKS = 0, 288, 592, 880, 1168, 1456, 1744
STRIP = 16 * Z
LAG_E, LAG_H = 6, 4


def iota(shape, dim):
    return lax.broadcasted_iota(I32, shape, dim)


class Copies:
    def __init__(self, sems):
        self.sems, self.used, self.open = sems, 0, []

    def start(self, source, target):
        copy = pltpu.make_async_copy(source, target, self.sems.at[self.used])
        self.used += 1
        copy.start()
        self.open.append(copy)

    def group(self):
        group, self.open = self.open, []
        return group

    def wait(self, group=None):
        for copy in self.group() if group is None else group:
            copy.wait()


def port_means(mean, cells):
    pick_y = (iota((Y, SLOTS), 0) == cells % Y).astype(F32)
    columns = jnp.dot(mean, pick_y, precision=HIGH, preferred_element_type=F32)
    return jnp.sum(jnp.where(iota((X, SLOTS), 0) == cells // Y, columns, 0.0), axis=0, keepdims=True)


def drawn_lanes(output_ref, state):
    lane, model = iota((MODELS, Y), 1), iota((MODELS, Y), 0)
    row = jnp.zeros((1, Y), F32)
    for q in range(2):
        drawn = jnp.sum(output_ref[:, q, :] * state, axis=1, keepdims=True)
        row = row + jnp.sum(
            jnp.where(lane == LANE_O + 2 * model + q, drawn, 0.0), axis=0, keepdims=True
        )
    return row


def pack_rows(read, up_ref, down_ref, c):
    low = iota((8, Y), 0) < 4
    for z in range(Z // 2):
        a, b = read(z), read(z + Z // 2)
        up_ref[16 * c + z] = jnp.where(low, a[:8], pltpu.roll(b[:8], 4, 0))
        down_ref[16 * c + z] = jnp.where(low, pltpu.roll(b[8:], 4, 0), a[8:])


def load_parts(copies, e_hbm, h_hbm, loss_hbm, gain_hbm, parts):
    sources = [e_hbm.at[c] for c in range(3)] + [h_hbm.at[c] for c in range(3)] + [loss_hbm, gain_hbm]
    groups = []
    for c, source in enumerate(sources):
        copies.start(source, parts.at[c])
        groups.append(copies.group())
    return groups


def pack_kernel(e_hbm, h_hbm, loss_hbm, gain_hbm, up_out, down_out, parts, up, down, sems):
    copies = Copies(sems)
    groups = load_parts(copies, e_hbm, h_hbm, loss_hbm, gain_hbm, parts)
    for c in range(8):
        copies.wait(groups[c])
        pack_rows(lambda z: parts[c, z], up, down, c)
        own = pl.ds(16 * c, 16)
        copies.start(up.at[own], up_out.at[own])
        copies.start(down.at[own], down_out.at[own])
    copies.wait()


def row_kernel(
    feed_hbm, e_hbm, cells_hbm, state_hbm, output_hbm, after_hbm, row_out, fixed_out,
    feed, ez, cells, state, output, line, row, fixed, sems,
):
    copies = Copies(sems)
    pairs = ((feed_hbm, feed), (e_hbm.at[2], ez), (cells_hbm, cells), (state_hbm, state), (output_hbm, output))
    for source, target in pairs:
        copies.start(source, target)
    copies.wait()
    mean = ez[0]
    for z in range(1, Z):
        mean = mean + ez[z]
    line[...] = jnp.zeros_like(line)
    line[0:1, :SLOTS] = cells[...].astype(F32)
    for k in range(4):
        line[k + 1 : k + 2, :MODELS] = feed[k // 2, k % 2 : k % 2 + 1, :]
    lines = line[...]
    total = pltpu.roll(lines, LANE_C, 1)[0:1]
    for k in range(4):
        total = total + pltpu.roll(lines, LANE_D + 8 * k, 1)[k + 1 : k + 2]
    fixed[...] = total
    row[...] = jnp.broadcast_to(total + drawn_lanes(output, state[...]), row.shape)
    row[:, :SLOTS] = jnp.broadcast_to(port_means(mean * (1.0 / Z), cells[...]), (256, SLOTS))
    copies.start(row, row_out)
    copies.start(fixed, fixed_out)
    copies.wait()


def side_kernel(
    e_hbm, h_hbm, loss_hbm, gain_hbm, after_hbm, before_hbm, row_hbm, halo_out, pack_out,
    parts, after, before, halo, pack, sems,
):
    copies = Copies(sems)
    copies.start(after_hbm, after)
    copies.start(before_hbm, before)
    received = copies.group()
    groups = load_parts(copies, e_hbm, h_hbm, loss_hbm, gain_hbm, parts)
    copies.wait(received)
    low = iota((8, Y), 0) < 4
    group = iota((8, Y), 1) // 16
    for c in range(8):
        copies.wait(groups[c])
        for z in range(Z // 2):
            a, b = after[16 * c + z], before[16 * c + z]
            halo[c, z] = jnp.where(low, a, b)
            halo[c, z + Z // 2] = pltpu.roll(jnp.where(low, b, a), 4, 0)
        for part in range(4):
            total = [jnp.zeros((8, Y), F32)] * 3
            for zl in range(8):
                z = part * 8 + zl
                plane = parts[c, z]
                for i, tile in enumerate((plane[:8], plane[8:], halo[c, z])):
                    moved = pltpu.roll(tile, (16 * zl + 8) % Y, 1)
                    total[i] = jnp.where(group == zl, moved, total[i])
            for i in range(3):
                pack[c, 8 * i : 8 * i + 8, Y * part : Y * part + Y] = total[i]
        copies.start(pack.at[c], pack_out.at[c])
        copies.start(halo.at[c], halo_out.at[c])
    copies.wait()


def index_kernel(counts_hbm, perm_hbm, pick_out, mask_out, counts_ref, perm_ref, pick, mask, sems):
    copies = Copies(sems)
    copies.start(counts_hbm, counts_ref)
    copies.start(perm_hbm, perm_ref)
    copies.wait()
    me, fx, fy = lax.axis_index(ALL), lax.axis_index("fx"), lax.axis_index(("fy", "grp"))
    counts = counts_ref[...]
    starts = counts
    for width in (1, 2, 4, 8, 16, 32, 64, 128):
        starts = starts + jnp.where(iota((1, 256), 1) >= width, pltpu.roll(starts, width, 1), 0)
    starts = starts - counts
    number = iota((LIST, 1), 0)
    slot = number % SLOTS
    dx, dy = number // SLOTS // 3 - 1, number // SLOTS % 3 - 1
    inside = (fx + dx >= 0) & (fx + dx < 8) & (fy + dy >= 0) & (fy + dy < 32)
    tile = jnp.where(inside, me + 32 * dx + dy, -1)
    own = iota((LIST, 256), 1) == tile
    start = jnp.sum(jnp.where(own, starts, 0), axis=1, keepdims=True)
    count = jnp.sum(jnp.where(own, counts, 0), axis=1, keepdims=True)
    live = slot < count
    wanted = jnp.where(live, start + slot, -1)
    even = iota((32, Y), 1) % 2 == 0
    perm = perm_ref[...]
    mates = jnp.where(even, pltpu.roll(perm, Y - 1, 1), pltpu.roll(perm, 1, 1))
    position = jnp.zeros((LIST, Y), I32)
    partner = jnp.zeros((LIST, Y), I32)
    spot = iota((2 * MODELS, Y), 0)
    mine_at = me * 2 * MODELS + 2 * (spot % MODELS) + spot // MODELS
    mine = jnp.zeros((2 * MODELS, Y), I32)
    for r in range(32):
        row, mate = perm[r : r + 1], mates[r : r + 1]
        hit = row == wanted
        position = jnp.where(hit, iota((LIST, Y), 1) + Y * r, position)
        partner = jnp.where(hit, mate, partner)
        mine = jnp.where(iota((2 * MODELS, Y), 1) + Y * r == mine_at, row, mine)
    position = jnp.sum(position, axis=1, keepdims=True)
    partner = jnp.sum(partner, axis=1, keepdims=True)
    mine = jnp.sum(mine, axis=1, keepdims=True)
    ports = jnp.concatenate([partner, mine], axis=0)
    total = LIST + 2 * MODELS
    before = starts <= ports
    port_tile = jnp.sum(before.astype(I32), axis=1, keepdims=True) - 1
    port_start = jnp.max(jnp.where(before, starts, 0), axis=1, keepdims=True)
    port_slot = ports - port_start
    pick[:LIST] = own.astype(F32).astype(jnp.bfloat16)
    pick[LIST : LIST + total] = (iota((total, 256), 1) == port_tile).astype(F32).astype(jnp.bfloat16)
    pick[LIST + total :] = (iota((LIST, 256), 1) == position // 16).astype(F32).astype(jnp.bfloat16)
    lane = iota((LIST, Y), 1)
    q = position % 2
    model = position // 2 % MODELS
    on = live.astype(F32)
    mask[OWN:MATE] = jnp.where(lane == slot, on, 0.0)
    mask[MATE:DRAWN] = (iota((total, Y), 1) == port_slot).astype(F32)
    mask[DRAWN:SELF] = jnp.where(lane == LANE_O + 2 * model + q, on, 0.0)
    mask[SELF:CROSS] = jnp.where(lane == LANE_D + 24 * q + model, on, 0.0)
    mask[CROSS:CELL] = jnp.where(lane == LANE_D + 8 * (q + 1) + model, on, 0.0)
    mask[CELL:] = (lane == LANE_C + slot).astype(F32)
    copies.start(pick, pick_out)
    copies.start(mask, mask_out)
    copies.wait()


def port_sources(gathered_ref, pick_ref, mask_ref):
    gathered = gathered_ref[...]
    high = gathered.astype(jnp.bfloat16)
    left_over = gathered - high.astype(F32)
    middle = left_over.astype(jnp.bfloat16)
    low = (left_over - middle.astype(F32)).astype(jnp.bfloat16)
    picked = jnp.dot(
        pick_ref[...], jnp.concatenate([high, middle, low], axis=1), preferred_element_type=F32
    )
    picked = picked[:, :Y] + picked[:, Y : 2 * Y] + picked[:, 2 * Y :]
    total = LIST + 2 * MODELS

    def choose(part, mask):
        return jnp.sum(part * mask, axis=1, keepdims=True)

    of_tile, of_port, of_model = picked[:LIST], picked[LIST : LIST + total], picked[LIST + total :]
    own = choose(of_tile, mask_ref[OWN:MATE])
    others = choose(of_port, mask_ref[MATE:DRAWN])
    mate, mine = others[:LIST], others[LIST:]
    current = choose(
        of_model, mask_ref[DRAWN:SELF] + mask_ref[SELF:CROSS] * own + mask_ref[CROSS:CELL] * mate
    )
    cell = choose(of_tile, mask_ref[CELL:]).astype(I32)
    number = iota((LIST, 1), 0) // SLOTS
    x = (number // 3 - 1) * X + cell // Y
    y = (number % 3 - 1) * Y + cell % Y
    lane = iota((LIST, 2 * Y), 1)
    lane_y = jnp.where(lane < Y, lane, jnp.where(lane < Y + 16, lane - 136, jnp.where(lane < Y + 32, lane - 24, -1000)))
    row = iota((LIST, Y), 1)
    row_x = jnp.where(row < 20, row, jnp.where(row < 24, row - 24, -1000))
    spread = jnp.where(lane_y == y, current, 0.0)
    to_row = (row_x == x).astype(F32)
    source = lax.dot_general(
        to_row, spread, (((0,), (0,)), ((), ())), precision=HIGH, preferred_element_type=F32
    )[:24]
    return source, mine


def repeat_groups(row_lanes):
    value = jnp.where(iota(row_lanes.shape, 1) < 16, row_lanes, 0.0)
    for width in (16, 32, 64):
        value = value + pltpu.roll(value, width, 1)
    return jnp.concatenate([value] * 4, axis=1)


def strip_step(fields, loss, gain, drive, keep_x, z_first, z_last):
    ex, ey, ez, hx, hy, hz = fields

    def up(v):
        return jnp.where(z_last, 0.0, pltpu.roll(v, STRIP - 16, 1))

    def down(v):
        return jnp.where(z_first, 0.0, pltpu.roll(v, 16, 1))

    hx = hx - COURANT * ((pltpu.roll(ez, STRIP - 1, 1) - ez) - (up(ey) - ey))
    hy = (hy - COURANT * ((up(ex) - ex) - (pltpu.roll(ez, 23, 0) - ez))) * keep_x
    hz = (hz - COURANT * ((pltpu.roll(ey, 23, 0) - ey) - (pltpu.roll(ex, STRIP - 1, 1) - ex))) * keep_x
    ex = loss * ex + gain * ((hz - pltpu.roll(hz, 1, 1)) - (hy - down(hy)))
    ey = loss * ey + gain * ((hx - down(hx)) - (hz - pltpu.roll(hz, 1, 0)))
    ez = loss * ez + gain * ((hy - pltpu.roll(hy, 1, 0)) - (hx - pltpu.roll(hx, 1, 1)) - drive)
    return [ex, ey, ez, hx, hy, hz]


def block_kernel(last, *refs):
    refs = list(refs)

    def take(n):
        got = refs[:n]
        del refs[:n]
        return got

    e_hbm, h_hbm, loss_hbm, gain_hbm, halo_hbm = take(5)
    packs_hbm = take(3)
    shared_hbm = take(8)
    if last:
        strips_hbm, after_hbm, before_hbm = take(3)
    e_out, h_out, state_out = take(3)
    if not last:
        row_out, up_out, down_out, strips_out = take(4)
    state, coef, seam, strips = take(4)
    packs = take(3)
    gathered, pick, mask, cells, fixed, moved, inputs, output = take(8)
    row, up, down, new_state, sems = take(5)
    fx, fy = lax.axis_index("fx"), lax.axis_index(("fy", "grp"))

    copies = Copies(sems)
    for source, target in zip(shared_hbm, (gathered, pick, mask, cells, fixed, moved, inputs, output)):
        copies.start(source, target)
    shared = copies.group()
    if last:
        for source, target in zip(packs_hbm, packs):
            copies.start(source.at[pl.ds(6, 2)], target.at[pl.ds(6, 2)])
        copies.start(strips_hbm, strips.at[:, pl.ds(0, X)])
        copies.start(after_hbm, up)
        copies.start(before_hbm, down)
    else:
        for source, target in zip(packs_hbm, packs):
            copies.start(source, target)
    edges = copies.group()
    for c in range(3):
        copies.start(e_hbm.at[c], state.at[c, pl.ds(0, Z), pl.ds(0, X)])
        copies.start(h_hbm.at[c], state.at[3 + c, pl.ds(1, Z), pl.ds(0, X)])
    copies.start(loss_hbm, coef.at[0, :, pl.ds(0, X)])
    copies.start(gain_hbm, coef.at[1, :, pl.ds(0, X)])
    for i in range(2):
        copies.start(halo_hbm.at[6 + i], coef.at[i, :, pl.ds(X, 8)])
    if not last:
        for c in range(6):
            copies.start(halo_hbm.at[c], state.at[c, pl.ds(c // 3, Z), pl.ds(X, 8)])
    fields = copies.group()
    for c in range(3):
        state[c, Z] = jnp.zeros((24, Y), F32)
        state[3 + c, 0] = jnp.zeros((24, Y), F32)
    copies.wait(shared)
    source, mine = port_sources(gathered, pick, mask)
    new_state[...] = (
        moved[...] + inputs[:, 0, :] * mine[:MODELS] + inputs[:, 1, :] * mine[MODELS:]
    )
    copies.start(new_state, state_out)
    copies.wait(edges)

    own, left, right = packs
    lanes = iota((24, STRIP), 1)
    before_half = lanes % 16 < 8
    low_coefs = [jnp.where(before_half, left[c], own[c]) for c in (6, 7)]
    high_coefs = [jnp.where(before_half, own[c], right[c]) for c in (6, 7)]
    if last:
        low = iota((8, Y), 0) < 4
        for c in range(6):
            for z in range(Z // 2):
                a, b = up[16 * c + z], down[16 * c + z]
                state[c, z + c // 3, X:] = jnp.where(low, a, b)
                state[c, z + Z // 2 + c // 3, X:] = pltpu.roll(jnp.where(low, b, a), 4, 0)
        for i in range(12):
            for j in range(2):
                a, b = up[96 + 2 * i + j], down[96 + 2 * i + j]
                strips[i, X:, Y * j : Y * j + Y] = jnp.where(low, a, b)
                strips[i, X:, Y * (j + 2) : Y * (j + 3)] = pltpu.roll(jnp.where(low, b, a), 4, 0)
    else:
        for c in range(6):
            strips[c] = jnp.where(before_half, left[c], own[c])
            strips[6 + c] = jnp.where(before_half, own[c], right[c])

    keep_x = jnp.where((iota((24, 1), 0) >= 20) & (fx == 0), 0.0, 1.0)
    keep_y = jnp.where(fy == 0, 0.0, 1.0)
    z_last, z_first = lanes >= STRIP - 16, lanes < 16
    at_seam = lanes % 16 == 8
    low_drive = repeat_groups(source[:, Y:])
    high_drive = repeat_groups(pltpu.roll(source[:, Y:], Y - 16, 1))

    def strips_step(s, carry):
        low_next = strip_step(
            [strips[c] for c in range(6)], *low_coefs, low_drive, keep_x, z_first, z_last
        )
        for i, (e_at, h_at) in enumerate(((2, 3), (0, 5))):
            joined = jnp.where(at_seam, strips[6 + e_at], pltpu.roll(low_next[h_at] * keep_y, 2, 1))
            for part in range(4):
                seam[s, i, part] = joined[:, Y * part : Y * part + Y]
        high_next = strip_step(
            [strips[6 + c] for c in range(6)], *high_coefs, high_drive, keep_x, z_first, z_last
        )
        for c in range(6):
            strips[c] = low_next[c]
            strips[6 + c] = high_next[c]
        return carry

    lax.fori_loop(0, K, strips_step, 0)

    if not last:
        copies.start(strips.at[:, pl.ds(0, X)], strips_out)
        low = iota((8, Y), 0) < 4
        for i in range(12):
            for j in range(2):
                a, b = (strips[i, :X, Y * k : Y * k + Y] for k in (j, j + 2))
                up[96 + 2 * i + j] = jnp.where(low, a[:8], pltpu.roll(b[:8], 4, 0))
                down[96 + 2 * i + j] = jnp.where(low, pltpu.roll(b[8:], 4, 0), a[8:])
    copies.wait(fields)

    main_source = source[:, :Y]
    lane = iota((24, Y), 1)
    end, begin = lane == Y - 1, lane == 0

    def step(s, carry):
        def turned(z):
            turn = (247 - 16 * (z % 8)) % Y
            return pltpu.roll(seam[s, 0, z // 8], turn, 1), pltpu.roll(seam[s, 1, z // 8], turn, 1)

        def shift_electric(z):
            seam_a, seam_b = turned(z)
            return (
                jnp.where(end, seam_a, pltpu.roll(state[2, z], Y - 1, 1)),
                jnp.where(end, seam_b, pltpu.roll(state[0, z], Y - 1, 1)),
                seam_a,
                seam_b,
            )

        def magnetic(z, ez_next, ex_next, seam_a, seam_b):
            ex, ey, ez = state[0, z], state[1, z], state[2, z]
            hx = state[3, z + 1] - COURANT * ((ez_next - ez) - (state[1, z + 1] - ey))
            hy = state[4, z + 1] - COURANT * ((state[0, z + 1] - ex) - (pltpu.roll(ez, 23, 0) - ez))
            hz = state[5, z + 1] - COURANT * ((pltpu.roll(ey, 23, 0) - ey) - (ex_next - ex))
            hy = hy * keep_x
            hz = hz * keep_x
            state[3, z + 1] = hx
            state[4, z + 1] = hy
            state[5, z + 1] = hz
            return (
                jnp.where(begin, seam_a, pltpu.roll(hx, 1, 1)),
                jnp.where(begin, seam_b, pltpu.roll(hz, 1, 1)),
            )

        def electric(z, hx_before, hz_before):
            hx, hy, hz = state[3, z + 1], state[4, z + 1], state[5, z + 1]
            loss, gain = coef[0, z], coef[1, z]
            state[0, z] = loss * state[0, z] + gain * ((hz - hz_before) - (hy - state[4, z]))
            state[1, z] = loss * state[1, z] + gain * (
                (hx - state[3, z]) - (hz - pltpu.roll(hz, 1, 0))
            )
            state[2, z] = loss * state[2, z] + gain * (
                (hy - pltpu.roll(hy, 1, 0)) - (hx - hx_before) - main_source
            )

        shifted, magnetics = {}, {}
        for t in range(Z + LAG_E + LAG_H):
            if t < Z:
                shifted[t] = shift_electric(t)
            if 0 <= t - LAG_E < Z:
                magnetics[t - LAG_E] = magnetic(t - LAG_E, *shifted.pop(t - LAG_E))
            if 0 <= t - LAG_E - LAG_H:
                electric(t - LAG_E - LAG_H, *magnetics.pop(t - LAG_E - LAG_H))
        return carry

    lax.fori_loop(0, K, step, 0)

    for c in range(3):
        copies.start(state.at[c, pl.ds(0, Z), pl.ds(0, X)], e_out.at[c])
        copies.start(state.at[3 + c, pl.ds(1, Z), pl.ds(0, X)], h_out.at[c])
    if not last:
        for c in range(6):
            pack_rows(lambda z: state[c, z + c // 3, :X], up, down, c)
        copies.start(up, up_out)
        copies.start(down, down_out)
        mean = state[2, 0, :X]
        for z in range(1, Z):
            mean = mean + state[2, z, :X]
        row[...] = jnp.broadcast_to(fixed[...] + drawn_lanes(output, new_state[...]), row.shape)
        row[:, :SLOTS] = jnp.broadcast_to(port_means(mean * (1.0 / Z), cells[...]), (256, SLOTS))
        copies.start(row, row_out)
    copies.wait()


def shape(*dims, dtype=F32):
    return jax.ShapeDtypeStruct(dims, dtype)


def call(kernel, outs, scratch, cost=1_000_000):
    scratch = [pltpu.VMEM(dims, F32) if isinstance(dims, tuple) else dims for dims in scratch]
    place = pl.BlockSpec(memory_space=pl.ANY)

    def run(*args):
        return pl.pallas_call(
            kernel,
            out_shape=outs,
            in_specs=[place] * len(args),
            out_specs=jax.tree.map(lambda _: place, outs),
            scratch_shapes=scratch + [pltpu.SemaphoreType.DMA((64,))],
            compiler_params=pltpu.CompilerParams(vmem_limit_bytes=56 * 1024 * 1024),
            cost_estimate=pl.CostEstimate(flops=cost, bytes_accessed=cost, transcendentals=0),
        )(*args)

    return run


def neighbours(up, down):
    after = lax.ppermute(up, "fx", [(i + 1, i) for i in range(7)])
    before = lax.ppermute(down, "fx", [(i, i + 1) for i in range(7)])
    return after, before


def sides(pack):
    axes = ("fy", "grp")
    left = lax.ppermute(pack, axes, [(i, i + 1) for i in range(31)])
    right = lax.ppermute(pack, axes, [(i + 1, i) for i in range(31)])
    return left, right


def exchange(row):
    return lax.all_to_all(row, ALL, 0, 0, tiled=True)


def body(
    efield, hfield, loss, gain, port_count, port_perm, port_cell,
    pole_state, transition, input_map, output_map, feedthrough,
):
    inputs = jnp.swapaxes(input_map, 1, 2)
    feed = jnp.transpose(feedthrough, (1, 2, 0))
    ints = functools.partial(pltpu.VMEM, dtype=I32)
    picks = 2 * LIST + LIST + 2 * MODELS
    tiles8, tiles6 = (128, 8, Y), (120, 8, Y)

    up, down = call(
        pack_kernel, (shape(*tiles8), shape(*tiles8)), [(8, Z, X, Y), tiles8, tiles8]
    )(efield, hfield, loss, gain)
    after, before = neighbours(up, down)
    row, fixed = call(
        row_kernel,
        (shape(256, Y), shape(1, Y)),
        [(2, 2, MODELS), (Z, X, Y), ints((1, SLOTS)), (MODELS, 256), (MODELS, 2, 256), (8, Y), (256, Y), (1, Y)],
    )(feed, efield, port_cell, pole_state, output_map, up)
    gathered = exchange(row)
    pick, mask = call(
        index_kernel,
        (shape(picks, 256, dtype=jnp.bfloat16), shape(MASKS, Y)),
        [ints((1, 256)), ints((32, Y)), pltpu.VMEM((picks, 256), jnp.bfloat16), (MASKS, Y)],
    )(port_count.reshape(1, 256), port_perm.reshape(32, Y))
    halo, pack = call(
        side_kernel,
        (shape(8, Z, 8, Y), shape(8, 24, STRIP)),
        [(8, Z, X, Y), tiles8, tiles8, (8, Z, 8, Y), (8, 24, STRIP)],
    )(efield, hfield, loss, gain, after, before, row)
    left, right = sides(pack)
    moved = jnp.einsum("mpr,mr->mp", transition, pole_state, precision=HIGH)

    scratch = (
        [(6, Z + 1, 24, Y), (2, Z, 24, Y), (K, 2, 4, 24, Y), (12, 24, STRIP)]
        + [(8, 24, STRIP)] * 3
        + [(256, Y), pltpu.VMEM((picks, 256), jnp.bfloat16), (MASKS, Y), ints((1, SLOTS)), (1, Y)]
        + [(MODELS, 256), (MODELS, 2, 256), (MODELS, 2, 256), (256, Y), tiles6, tiles6, (MODELS, 256)]
    )
    field = (shape(3, Z, X, Y), shape(3, Z, X, Y), shape(MODELS, 256))
    electric, magnetic, state, row, up, down, strips = call(
        functools.partial(block_kernel, False),
        field + (shape(256, Y), shape(*tiles6), shape(*tiles6), shape(12, X, STRIP)),
        scratch,
    )(
        efield, hfield, loss, gain, halo, pack, left, right,
        gathered, pick, mask, port_cell, fixed, moved, inputs, output_map,
    )

    after, before = neighbours(up, down)
    gathered = exchange(row)
    moved = jnp.einsum("mpr,mr->mp", transition, state, precision=HIGH)
    return call(functools.partial(block_kernel, True), field, scratch)(
        electric, magnetic, loss, gain, halo, pack, left, right,
        gathered, pick, mask, port_cell, fixed, moved, inputs, output_map, strips, after, before,
    )


def solution(mesh):
    return jax.shard_map(
        body,
        mesh=mesh,
        in_specs=(
            P(None, None, "fx", ("fy", "grp")),
            P(None, None, "fx", ("fy", "grp")),
            P(None, "fx", ("fy", "grp")),
            P(None, "fx", ("fy", "grp")),
            P(),
            P(),
            P(ALL, None),
            P(ALL, None),
            P(ALL, None, None),
            P(ALL, None, None),
            P(ALL, None, None),
            P(ALL, None, None),
        ),
        out_specs=(
            P(None, None, "fx", ("fy", "grp")),
            P(None, None, "fx", ("fy", "grp")),
            P(ALL, None),
        ),
        check_vma=False,
    )
```

```python
import functools

import jax
import jax.numpy as jnp
from jax import lax
from jax.experimental import pallas as pl
from jax.experimental.pallas import tpu as pltpu
from jax.sharding import PartitionSpec as P

K = 4
BLOCKS = 2
COURANT = 0.5
HIGH = lax.Precision.HIGHEST
ALL = ("fx", "fy", "grp")
Z, X, Y = 32, 16, 128
SLOTS = 32
LIST = 9 * SLOTS
MODELS = 8
F32 = jnp.float32
I32 = jnp.int32
LANE_O, LANE_D, LANE_C = 32, 48, 80
OWN, MATE, DRAWN, SELF, CROSS, CELL, MASKS = 0, 288, 592, 880, 1168, 1456, 1744
STRIP = 16 * Z
LAG_E, LAG_H = 6, 4


def iota(shape, dim):
    return lax.broadcasted_iota(I32, shape, dim)


class Copies:
    def __init__(self, sems):
        self.sems, self.used, self.open = sems, 0, []

    def start(self, source, target):
        copy = pltpu.make_async_copy(source, target, self.sems.at[self.used])
        self.used += 1
        copy.start()
        self.open.append(copy)

    def group(self):
        group, self.open = self.open, []
        return group

    def wait(self, group=None):
        for copy in self.group() if group is None else group:
            copy.wait()


def port_means(mean, cells):
    pick_y = (iota((Y, SLOTS), 0) == cells % Y).astype(F32)
    columns = jnp.dot(mean, pick_y, precision=HIGH, preferred_element_type=F32)
    return jnp.sum(jnp.where(iota((X, SLOTS), 0) == cells // Y, columns, 0.0), axis=0, keepdims=True)


def drawn_lanes(output_ref, state):
    lane, model = iota((MODELS, Y), 1), iota((MODELS, Y), 0)
    row = jnp.zeros((1, Y), F32)
    for q in range(2):
        drawn = jnp.sum(output_ref[:, q, :] * state, axis=1, keepdims=True)
        row = row + jnp.sum(
            jnp.where(lane == LANE_O + 2 * model + q, drawn, 0.0), axis=0, keepdims=True
        )
    return row


def pack_rows(read, up_ref, down_ref, c):
    low = iota((8, Y), 0) < 4
    for z in range(Z // 2):
        a, b = read(z), read(z + Z // 2)
        up_ref[16 * c + z] = jnp.where(low, a[:8], pltpu.roll(b[:8], 4, 0))
        down_ref[16 * c + z] = jnp.where(low, pltpu.roll(b[8:], 4, 0), a[8:])


def load_parts(copies, e_hbm, h_hbm, loss_hbm, gain_hbm, parts):
    sources = [e_hbm.at[c] for c in range(3)] + [h_hbm.at[c] for c in range(3)] + [loss_hbm, gain_hbm]
    groups = []
    for c, source in enumerate(sources):
        copies.start(source, parts.at[c])
        groups.append(copies.group())
    return groups


def first_kernel(
    e_hbm, h_hbm, loss_hbm, gain_hbm, feed_hbm, cells_hbm, state_hbm, output_hbm,
    even_out, odd_out, row_out, fixed_out,
    parts, feed, cells, state, output, sent, line, row, fixed, sems,
):
    copies = Copies(sems)
    groups = load_parts(copies, e_hbm, h_hbm, loss_hbm, gain_hbm, parts)
    for origin, target in ((feed_hbm, feed), (cells_hbm, cells), (state_hbm, state), (output_hbm, output)):
        copies.start(origin, target)
    small = copies.group()
    odd = lax.axis_index("fx") % 2
    for c in range(8):
        copies.wait(groups[c])
        pack_rows(lambda z: parts[c, z], sent.at[1 - odd], sent.at[odd], c)
        own = pl.ds(16 * c, 16)
        copies.start(sent.at[0, own], even_out.at[own])
        copies.start(sent.at[1, own], odd_out.at[own])
    copies.wait(small)
    mean = parts[2, 0]
    for z in range(1, Z):
        mean = mean + parts[2, z]
    line[...] = jnp.zeros_like(line)
    line[0:1, :SLOTS] = cells[...].astype(F32)
    for k in range(4):
        line[k + 1 : k + 2, :MODELS] = feed[k // 2, k % 2 : k % 2 + 1, :]
    lines = line[...]
    total = pltpu.roll(lines, LANE_C, 1)[0:1]
    for k in range(4):
        total = total + pltpu.roll(lines, LANE_D + 8 * k, 1)[k + 1 : k + 2]
    fixed[...] = total
    row[...] = jnp.broadcast_to(total + drawn_lanes(output, state[...]), row.shape)
    row[:, :SLOTS] = jnp.broadcast_to(port_means(mean * (1.0 / Z), cells[...]), (256, SLOTS))
    copies.start(row, row_out)
    copies.start(fixed, fixed_out)
    copies.wait()


def side_kernel(
    e_hbm, h_hbm, loss_hbm, gain_hbm, even_hbm, odd_hbm, halo_out, pack_out, even_out, odd_out,
    parts, got, halo, pack, sent, sems,
):
    copies = Copies(sems)
    copies.start(even_hbm, got.at[0])
    copies.start(odd_hbm, got.at[1])
    received = copies.group()
    odd = lax.axis_index("fx") % 2
    after, before = got.at[odd], got.at[1 - odd]
    odd = lax.axis_index(("fy", "grp")) % 2
    to_right, to_left = sent.at[odd], sent.at[1 - odd]
    groups = load_parts(copies, e_hbm, h_hbm, loss_hbm, gain_hbm, parts)
    copies.wait(received)
    low = iota((8, Y), 0) < 4
    group = iota((8, Y), 1) // 16
    half = iota((8, Y), 1) % 16 < 8
    for c in range(8):
        copies.wait(groups[c])
        for z in range(Z // 2):
            a, b = after[16 * c + z], before[16 * c + z]
            halo[c, z] = jnp.where(low, a, b)
            halo[c, z + Z // 2] = pltpu.roll(jnp.where(low, b, a), 4, 0)
        totals = []
        for part in range(4):
            total = [jnp.zeros((8, Y), F32)] * 3
            for zl in range(8):
                z = part * 8 + zl
                plane = parts[c, z]
                for i, tile in enumerate((plane[:8], plane[8:], halo[c, z])):
                    moved = pltpu.roll(tile, (16 * zl + 8) % Y, 1)
                    total[i] = jnp.where(group == zl, moved, total[i])
            totals.append(total)
            for i in range(3):
                pack[c, 8 * i : 8 * i + 8, Y * part : Y * part + Y] = total[i]
        for pair in range(2):
            for i in range(3):
                a, b = totals[2 * pair][i], totals[2 * pair + 1][i]
                rows, lanes = slice(8 * i, 8 * i + 8), slice(Y * pair, Y * pair + Y)
                to_right[c, rows, lanes] = jnp.where(half, a, pltpu.roll(b, 8, 1))
                to_left[c, rows, lanes] = jnp.where(half, pltpu.roll(a, Y - 8, 1), b)
        copies.start(pack.at[c], pack_out.at[c])
        copies.start(sent.at[0, c], even_out.at[c])
        copies.start(sent.at[1, c], odd_out.at[c])
        copies.start(halo.at[c], halo_out.at[c])
    copies.wait()


def index_kernel(
    counts_hbm, perm_hbm, gathered_hbm, moved_hbm, inputs_hbm, output_hbm, fixed_hbm,
    pick_out, mask_out, source_out, state_out, line_out,
    counts_ref, perm_ref, gathered, moved, inputs, output, fixed, pick, mask, source, new_state, line, sems,
):
    copies = Copies(sems)
    copies.start(counts_hbm, counts_ref)
    copies.start(perm_hbm, perm_ref)
    early = copies.group()
    pairs = ((gathered_hbm, gathered), (moved_hbm, moved), (inputs_hbm, inputs), (output_hbm, output), (fixed_hbm, fixed))
    for origin, target in pairs:
        copies.start(origin, target)
    late = copies.group()
    copies.wait(early)
    me, fx, fy = lax.axis_index(ALL), lax.axis_index("fx"), lax.axis_index(("fy", "grp"))
    counts = counts_ref[...]
    starts = counts
    for width in (1, 2, 4, 8, 16, 32, 64, 128):
        starts = starts + jnp.where(iota((1, 256), 1) >= width, pltpu.roll(starts, width, 1), 0)
    starts = starts - counts
    number = iota((LIST, 1), 0)
    slot = number % SLOTS
    dx, dy = number // SLOTS // 3 - 1, number // SLOTS % 3 - 1
    inside = (fx + dx >= 0) & (fx + dx < 8) & (fy + dy >= 0) & (fy + dy < 32)
    tile = jnp.where(inside, me + 32 * dx + dy, -1)
    own = iota((LIST, 256), 1) == tile
    start = jnp.sum(jnp.where(own, starts, 0), axis=1, keepdims=True)
    count = jnp.sum(jnp.where(own, counts, 0), axis=1, keepdims=True)
    live = slot < count
    wanted = jnp.where(live, start + slot, -1)
    even = iota((32, Y), 1) % 2 == 0
    perm = perm_ref[...]
    mates = jnp.where(even, pltpu.roll(perm, Y - 1, 1), pltpu.roll(perm, 1, 1))
    position = jnp.zeros((LIST, Y), I32)
    partner = jnp.zeros((LIST, Y), I32)
    spot = iota((2 * MODELS, Y), 0)
    mine_at = me * 2 * MODELS + 2 * (spot % MODELS) + spot // MODELS
    mine = jnp.zeros((2 * MODELS, Y), I32)
    for r in range(32):
        row, mate = perm[r : r + 1], mates[r : r + 1]
        hit = row == wanted
        position = jnp.where(hit, iota((LIST, Y), 1) + Y * r, position)
        partner = jnp.where(hit, mate, partner)
        mine = jnp.where(iota((2 * MODELS, Y), 1) + Y * r == mine_at, row, mine)
    position = jnp.sum(position, axis=1, keepdims=True)
    partner = jnp.sum(partner, axis=1, keepdims=True)
    mine = jnp.sum(mine, axis=1, keepdims=True)
    ports = jnp.concatenate([partner, mine], axis=0)
    total = LIST + 2 * MODELS
    before = starts <= ports
    port_tile = jnp.sum(before.astype(I32), axis=1, keepdims=True) - 1
    port_start = jnp.max(jnp.where(before, starts, 0), axis=1, keepdims=True)
    port_slot = ports - port_start
    pick[:LIST] = own.astype(F32).astype(jnp.bfloat16)
    pick[LIST : LIST + total] = (iota((total, 256), 1) == port_tile).astype(F32).astype(jnp.bfloat16)
    pick[LIST + total :] = (iota((LIST, 256), 1) == position // 16).astype(F32).astype(jnp.bfloat16)
    lane = iota((LIST, Y), 1)
    q = position % 2
    model = position // 2 % MODELS
    on = live.astype(F32)
    mask[OWN:MATE] = jnp.where(lane == slot, on, 0.0)
    mask[MATE:DRAWN] = (iota((total, Y), 1) == port_slot).astype(F32)
    mask[DRAWN:SELF] = jnp.where(lane == LANE_O + 2 * model + q, on, 0.0)
    mask[SELF:CROSS] = jnp.where(lane == LANE_D + 24 * q + model, on, 0.0)
    mask[CROSS:CELL] = jnp.where(lane == LANE_D + 8 * (q + 1) + model, on, 0.0)
    mask[CELL:] = (lane == LANE_C + slot).astype(F32)
    copies.start(pick, pick_out)
    copies.start(mask, mask_out)
    copies.wait(late)
    source[...], mine = port_sources(gathered, pick, mask)
    new_state[...] = moved[...] + input_part(inputs, mine)
    line[...] = fixed[...] + drawn_lanes(output, new_state[...])
    copies.start(source, source_out)
    copies.start(new_state, state_out)
    copies.start(line, line_out)
    copies.wait()


def port_sources(gathered_ref, pick_ref, mask_ref):
    gathered = gathered_ref[...]
    high = gathered.astype(jnp.bfloat16)
    left_over = gathered - high.astype(F32)
    middle = left_over.astype(jnp.bfloat16)
    low = (left_over - middle.astype(F32)).astype(jnp.bfloat16)
    picked = jnp.dot(
        pick_ref[...], jnp.concatenate([high, middle, low], axis=1), preferred_element_type=F32
    )
    picked = picked[:, :Y] + picked[:, Y : 2 * Y] + picked[:, 2 * Y :]
    total = LIST + 2 * MODELS

    def choose(part, mask):
        return jnp.sum(part * mask, axis=1, keepdims=True)

    of_tile, of_port, of_model = picked[:LIST], picked[LIST : LIST + total], picked[LIST + total :]
    own = choose(of_tile, mask_ref[OWN:MATE])
    others = choose(of_port, mask_ref[MATE:DRAWN])
    mate, mine = others[:LIST], others[LIST:]
    current = choose(
        of_model, mask_ref[DRAWN:SELF] + mask_ref[SELF:CROSS] * own + mask_ref[CROSS:CELL] * mate
    )
    cell = choose(of_tile, mask_ref[CELL:]).astype(I32)
    number = iota((LIST, 1), 0) // SLOTS
    x = (number // 3 - 1) * X + cell // Y
    y = (number % 3 - 1) * Y + cell % Y
    lane = iota((LIST, 2 * Y), 1)
    lane_y = jnp.where(lane < Y, lane, jnp.where(lane < Y + 16, lane - 136, jnp.where(lane < Y + 32, lane - 24, -1000)))
    row = iota((LIST, Y), 1)
    row_x = jnp.where(row < 20, row, jnp.where(row < 24, row - 24, -1000))
    spread = jnp.where(lane_y == y, current, 0.0)
    to_row = (row_x == x).astype(F32)
    source = lax.dot_general(
        to_row, spread, (((0,), (0,)), ((), ())), precision=HIGH, preferred_element_type=F32
    )[:24]
    return source, mine


def input_part(inputs, mine):
    return inputs[:, 0, :] * mine[:MODELS] + inputs[:, 1, :] * mine[MODELS:]


def repeat_groups(row_lanes):
    value = jnp.where(iota(row_lanes.shape, 1) < 16, row_lanes, 0.0)
    for width in (16, 32, 64):
        value = value + pltpu.roll(value, width, 1)
    return jnp.concatenate([value] * 4, axis=1)


def strip_step(fields, loss, gain, drive, keep_x, z_first, z_last):
    ex, ey, ez, hx, hy, hz = fields

    def up(v):
        return jnp.where(z_last, 0.0, pltpu.roll(v, STRIP - 16, 1))

    def down(v):
        return jnp.where(z_first, 0.0, pltpu.roll(v, 16, 1))

    hx = hx - COURANT * ((pltpu.roll(ez, STRIP - 1, 1) - ez) - (up(ey) - ey))
    hy = (hy - COURANT * ((up(ex) - ex) - (pltpu.roll(ez, 23, 0) - ez))) * keep_x
    hz = (hz - COURANT * ((pltpu.roll(ey, 23, 0) - ey) - (pltpu.roll(ex, STRIP - 1, 1) - ex))) * keep_x
    ex = loss * ex + gain * ((hz - pltpu.roll(hz, 1, 1)) - (hy - down(hy)))
    ey = loss * ey + gain * ((hx - down(hx)) - (hz - pltpu.roll(hz, 1, 0)))
    ez = loss * ez + gain * ((hy - pltpu.roll(hy, 1, 0)) - (hx - pltpu.roll(hx, 1, 1)) - drive)
    return [ex, ey, ez, hx, hy, hz]


def block_kernel(last, *refs):
    refs = list(refs)

    def take(n):
        got = refs[:n]
        del refs[:n]
        return got

    e_hbm, h_hbm, loss_hbm, gain_hbm, halo_hbm = take(5)
    if last:
        shared_hbm = take(4)
        shared_hbm += take(1)
        strips_hbm, edge_coefs_hbm, even_hbm, odd_hbm = take(4)
        e_out, h_out, state_out = take(3)
    else:
        shared_hbm = take(3)
        pack_hbm, even_hbm, odd_hbm = take(3)
        e_out, h_out, row_out, even_out, odd_out, strips_out, edge_coefs_out = take(7)
    state, coef, seam, strips, edge_coefs = take(5)
    shared = take(len(shared_hbm))
    if not last:
        pack, sent = take(2)
    got, result, sems = take(3)
    fx, fy = lax.axis_index("fx"), lax.axis_index(("fy", "grp"))

    copies = Copies(sems)
    for origin, target in zip(shared_hbm, shared):
        copies.start(origin, target)
    ready = copies.group()
    if last:
        copies.start(strips_hbm, strips.at[:, pl.ds(0, X)])
        copies.start(edge_coefs_hbm, edge_coefs)
        after, before = got.at[fx % 2], got.at[1 - fx % 2]
    else:
        copies.start(pack_hbm, pack)
        right, left = got.at[fy % 2], got.at[1 - fy % 2]
        up, down = sent.at[1 - fx % 2], sent.at[fx % 2]
    copies.start(even_hbm, got.at[0])
    copies.start(odd_hbm, got.at[1])
    edges = copies.group()
    for c in range(3):
        copies.start(e_hbm.at[c], state.at[c, pl.ds(0, Z), pl.ds(0, X)])
        copies.start(h_hbm.at[c], state.at[3 + c, pl.ds(1, Z), pl.ds(0, X)])
    copies.start(loss_hbm, coef.at[0, :, pl.ds(0, X)])
    copies.start(gain_hbm, coef.at[1, :, pl.ds(0, X)])
    for i in range(2):
        copies.start(halo_hbm.at[6 + i], coef.at[i, :, pl.ds(X, 8)])
    if not last:
        for c in range(6):
            copies.start(halo_hbm.at[c], state.at[c, pl.ds(c // 3, Z), pl.ds(X, 8)])
    fields = copies.group()
    for c in range(3):
        state[c, Z] = jnp.zeros((24, Y), F32)
        state[3 + c, 0] = jnp.zeros((24, Y), F32)
    copies.wait(ready)
    if last:
        pick, mask, moved, inputs, gathered = shared
        source, mine = port_sources(gathered, pick, mask)
        result[...] = moved[...] + input_part(inputs, mine)
        copies.start(result, state_out)
    else:
        source_ref, cells, line = shared
        source = source_ref[...]
    copies.wait(edges)

    lanes = iota((24, STRIP), 1)
    if last:
        low = iota((8, Y), 0) < 4
        for c in range(6):
            for z in range(Z // 2):
                a, b = after[16 * c + z], before[16 * c + z]
                state[c, z + c // 3, X:] = jnp.where(low, a, b)
                state[c, z + Z // 2 + c // 3, X:] = pltpu.roll(jnp.where(low, b, a), 4, 0)
        for i in range(12):
            for j in range(2):
                a, b = after[96 + 2 * i + j], before[96 + 2 * i + j]
                strips[i, X:, Y * j : Y * j + Y] = jnp.where(low, a, b)
                strips[i, X:, Y * (j + 2) : Y * (j + 3)] = pltpu.roll(jnp.where(low, b, a), 4, 0)
    else:
        half = iota((24, Y), 1) % 16 < 8
        for c in range(8):
            low_ref, high_ref = (strips.at[c], strips.at[6 + c]) if c < 6 else (edge_coefs.at[c - 6], edge_coefs.at[c - 4])
            for part in range(4):
                at, pair = slice(Y * part, Y * part + Y), slice(Y * (part // 2), Y * (part // 2) + Y)
                own, from_left, from_right = pack[c, :, at], left[c, :, pair], right[c, :, pair]
                if part % 2:
                    from_left = pltpu.roll(from_left, Y - 8, 1)
                else:
                    from_right = pltpu.roll(from_right, 8, 1)
                low_ref[:, at] = jnp.where(half, from_left, own)
                high_ref[:, at] = jnp.where(half, own, from_right)
        copies.start(edge_coefs, edge_coefs_out)

    keep_x = jnp.where((iota((24, 1), 0) >= 20) & (fx == 0), 0.0, 1.0)
    keep_y = jnp.where(fy == 0, 0.0, 1.0)
    z_last, z_first = lanes >= STRIP - 16, lanes < 16
    at_seam = lanes % 16 == 8
    low_drive = repeat_groups(source[:, Y:])
    high_drive = repeat_groups(pltpu.roll(source[:, Y:], Y - 16, 1))

    def strips_step(s, carry):
        low_next = strip_step(
            [strips[c] for c in range(6)], edge_coefs[0], edge_coefs[1], low_drive, keep_x, z_first, z_last
        )
        for i, (e_at, h_at) in enumerate(((2, 3), (0, 5))):
            joined = jnp.where(at_seam, strips[6 + e_at], pltpu.roll(low_next[h_at] * keep_y, 2, 1))
            for part in range(4):
                seam[s, i, part] = joined[:, Y * part : Y * part + Y]
        high_next = strip_step(
            [strips[6 + c] for c in range(6)], edge_coefs[2], edge_coefs[3], high_drive, keep_x, z_first, z_last
        )
        for c in range(6):
            strips[c] = low_next[c]
            strips[6 + c] = high_next[c]
        return carry

    lax.fori_loop(0, K, strips_step, 0)

    if not last:
        copies.start(strips.at[:, pl.ds(0, X)], strips_out)
        low = iota((8, Y), 0) < 4
        for i in range(12):
            for j in range(2):
                a, b = (strips[i, :X, Y * k : Y * k + Y] for k in (j, j + 2))
                up[96 + 2 * i + j] = jnp.where(low, a[:8], pltpu.roll(b[:8], 4, 0))
                down[96 + 2 * i + j] = jnp.where(low, pltpu.roll(b[8:], 4, 0), a[8:])
    copies.wait(fields)

    main_source = source[:, :Y]
    lane = iota((24, Y), 1)
    end, begin = lane == Y - 1, lane == 0

    def step(s, carry):
        def turned(z):
            turn = (247 - 16 * (z % 8)) % Y
            return pltpu.roll(seam[s, 0, z // 8], turn, 1), pltpu.roll(seam[s, 1, z // 8], turn, 1)

        def shift_electric(z):
            seam_a, seam_b = turned(z)
            return (
                jnp.where(end, seam_a, pltpu.roll(state[2, z], Y - 1, 1)),
                jnp.where(end, seam_b, pltpu.roll(state[0, z], Y - 1, 1)),
                seam_a,
                seam_b,
            )

        def magnetic(z, ez_next, ex_next, seam_a, seam_b):
            ex, ey, ez = state[0, z], state[1, z], state[2, z]
            hx = state[3, z + 1] - COURANT * ((ez_next - ez) - (state[1, z + 1] - ey))
            hy = state[4, z + 1] - COURANT * ((state[0, z + 1] - ex) - (pltpu.roll(ez, 23, 0) - ez))
            hz = state[5, z + 1] - COURANT * ((pltpu.roll(ey, 23, 0) - ey) - (ex_next - ex))
            hy = hy * keep_x
            hz = hz * keep_x
            state[3, z + 1] = hx
            state[4, z + 1] = hy
            state[5, z + 1] = hz
            return (
                jnp.where(begin, seam_a, pltpu.roll(hx, 1, 1)),
                jnp.where(begin, seam_b, pltpu.roll(hz, 1, 1)),
            )

        def electric(z, hx_before, hz_before):
            hx, hy, hz = state[3, z + 1], state[4, z + 1], state[5, z + 1]
            loss, gain = coef[0, z], coef[1, z]
            state[0, z] = loss * state[0, z] + gain * ((hz - hz_before) - (hy - state[4, z]))
            state[1, z] = loss * state[1, z] + gain * (
                (hx - state[3, z]) - (hz - pltpu.roll(hz, 1, 0))
            )
            state[2, z] = loss * state[2, z] + gain * (
                (hy - pltpu.roll(hy, 1, 0)) - (hx - hx_before) - main_source
            )

        shifted, magnetics = {}, {}
        for t in range(Z + LAG_E + LAG_H):
            if t < Z:
                shifted[t] = shift_electric(t)
            if 0 <= t - LAG_E < Z:
                magnetics[t - LAG_E] = magnetic(t - LAG_E, *shifted.pop(t - LAG_E))
            if 0 <= t - LAG_E - LAG_H:
                electric(t - LAG_E - LAG_H, *magnetics.pop(t - LAG_E - LAG_H))
        return carry

    lax.fori_loop(0, K, step, 0)

    for c in range(3):
        copies.start(state.at[c, pl.ds(0, Z), pl.ds(0, X)], e_out.at[c])
        copies.start(state.at[3 + c, pl.ds(1, Z), pl.ds(0, X)], h_out.at[c])
    if not last:
        for c in range(6):
            pack_rows(lambda z: state[c, z + c // 3, :X], up, down, c)
        copies.start(sent.at[0], even_out)
        copies.start(sent.at[1], odd_out)
        mean = state[2, 0, :X]
        for z in range(1, Z):
            mean = mean + state[2, z, :X]
        result[...] = jnp.broadcast_to(line[...], result.shape)
        result[:, :SLOTS] = jnp.broadcast_to(port_means(mean * (1.0 / Z), cells[...]), (256, SLOTS))
        copies.start(result, row_out)
    copies.wait()


def shape(*dims, dtype=F32):
    return jax.ShapeDtypeStruct(dims, dtype)


def call(kernel, outs, scratch, cost=1_000_000):
    scratch = [pltpu.VMEM(dims, F32) if isinstance(dims, tuple) else dims for dims in scratch]
    place = pl.BlockSpec(memory_space=pl.ANY)

    def run(*args):
        return pl.pallas_call(
            kernel,
            out_shape=outs,
            in_specs=[place] * len(args),
            out_specs=jax.tree.map(lambda _: place, outs),
            scratch_shapes=scratch + [pltpu.SemaphoreType.DMA((64,))],
            compiler_params=pltpu.CompilerParams(vmem_limit_bytes=56 * 1024 * 1024),
            cost_estimate=pl.CostEstimate(flops=cost, bytes_accessed=cost, transcendentals=0),
        )(*args)

    return run


def gate(values, received, other):
    def nothing(*refs):
        pass

    place = pl.BlockSpec(memory_space=pl.ANY)
    return pl.pallas_call(
        nothing,
        out_shape=[shape(*value.shape) for value in values],
        in_specs=[place] * (len(values) + 2),
        out_specs=[place] * len(values),
        input_output_aliases={i: i for i in range(len(values))},
    )(*values, received, other)


def neighbours(even, odd, axes, count):
    later = [(i, i + 1) for i in range(1, count - 1, 2)]
    return (
        lax.ppermute(even, axes, [(i, i ^ 1) for i in range(count)]),
        lax.ppermute(odd, axes, later + [(j, i) for i, j in later]),
    )


def exchange(row):
    return lax.all_to_all(row, ALL, 0, 0, tiled=True)


def body(
    efield, hfield, loss, gain, port_count, port_perm, port_cell,
    pole_state, transition, input_map, output_map, feedthrough,
):
    inputs = jnp.swapaxes(input_map, 1, 2)
    feed = jnp.transpose(feedthrough, (1, 2, 0))
    ints = functools.partial(pltpu.VMEM, dtype=I32)
    picks = 2 * LIST + LIST + 2 * MODELS
    tiles8, tiles6 = (128, 8, Y), (120, 8, Y)

    even, odd, row, fixed = call(
        first_kernel,
        (shape(*tiles8), shape(*tiles8), shape(256, Y), shape(1, Y)),
        [(8, Z, X, Y), (2, 2, MODELS), ints((1, SLOTS)), (MODELS, 256), (MODELS, 2, 256)]
        + [(2,) + tiles8, (8, Y), (256, Y), (1, Y)],
    )(efield, hfield, loss, gain, feed, port_cell, pole_state, output_map)
    even, odd = neighbours(even, odd, "fx", 8)
    gathered = exchange(row)
    ends = (8, 24, STRIP // 2)
    halo, pack, even, odd = call(
        side_kernel,
        (shape(8, Z, 8, Y), shape(8, 24, STRIP), shape(*ends), shape(*ends)),
        [(8, Z, X, Y), (2,) + tiles8, (8, Z, 8, Y), (8, 24, STRIP), (2,) + ends],
    )(efield, hfield, loss, gain, even, odd)
    moved = jnp.einsum("mpr,mr->mp", transition, pole_state, precision=HIGH)
    even, odd = gate((even, odd), gathered, moved)
    even, odd = neighbours(even, odd, ("fy", "grp"), 32)
    bits = pltpu.VMEM((picks, 256), jnp.bfloat16)
    pick, mask, source, state, line = call(
        index_kernel,
        (shape(picks, 256, dtype=jnp.bfloat16), shape(MASKS, Y), shape(24, 256), shape(MODELS, 256), shape(1, Y)),
        [ints((1, 256)), ints((32, Y)), (256, Y), (MODELS, 256), (MODELS, 2, 256), (MODELS, 2, 256), (1, Y)]
        + [bits, (MASKS, Y), (24, 256), (MODELS, 256), (1, Y)],
    )(port_count.reshape(1, 256), port_perm.reshape(32, Y), gathered, moved, inputs, output_map, fixed)

    scratch = [(6, Z + 1, 24, Y), (2, Z, 24, Y), (K, 2, 4, 24, Y), (12, 24, STRIP), (4, 24, STRIP)]
    field = (shape(3, Z, X, Y), shape(3, Z, X, Y))
    electric, magnetic, row, next_even, next_odd, strips, edge_coefs = call(
        functools.partial(block_kernel, False),
        field
        + (shape(256, Y), shape(*tiles6), shape(*tiles6), shape(12, X, STRIP), shape(4, 24, STRIP)),
        scratch + [(24, 256), ints((1, SLOTS)), (1, Y), (8, 24, STRIP), (2,) + tiles6, (2,) + ends, (256, Y)],
    )(efield, hfield, loss, gain, halo, source, port_cell, line, pack, even, odd)

    even, odd = neighbours(next_even, next_odd, "fx", 8)
    gathered = exchange(row)
    moved = jnp.einsum("mpr,mr->mp", transition, state, precision=HIGH)
    return call(
        functools.partial(block_kernel, True),
        field + (shape(MODELS, 256),),
        scratch
        + [bits, (MASKS, Y), (MODELS, 256), (MODELS, 2, 256), (256, Y), (2,) + tiles6, (MODELS, 256)],
    )(
        electric, magnetic, loss, gain, halo, pick, mask, moved, inputs,
        gathered, strips, edge_coefs, even, odd,
    )


def solution(mesh):
    return jax.shard_map(
        body,
        mesh=mesh,
        in_specs=(
            P(None, None, "fx", ("fy", "grp")),
            P(None, None, "fx", ("fy", "grp")),
            P(None, "fx", ("fy", "grp")),
            P(None, "fx", ("fy", "grp")),
            P(),
            P(),
            P(ALL, None),
            P(ALL, None),
            P(ALL, None, None),
            P(ALL, None, None),
            P(ALL, None, None),
            P(ALL, None, None),
        ),
        out_specs=(
            P(None, None, "fx", ("fy", "grp")),
            P(None, None, "fx", ("fy", "grp")),
            P(ALL, None),
        ),
        check_vma=False,
    )
```

```python
import functools

import jax
import jax.numpy as jnp
from jax import lax
from jax.experimental import pallas as pl
from jax.experimental.pallas import tpu as pltpu
from jax.sharding import PartitionSpec as P

K = 4
BLOCKS = 2
COURANT = 0.5
HIGH = lax.Precision.HIGHEST
ALL = ("fx", "fy", "grp")
Z, X, Y = 32, 16, 128
SLOTS = 32
LIST = 9 * SLOTS
MODELS = 8
F32 = jnp.float32
I32 = jnp.int32
LANE_O, LANE_D, LANE_C = 32, 48, 80
OWN, MATE, DRAWN, SELF, CROSS, CELL, MASKS = 0, 288, 592, 880, 1168, 1456, 1744
STRIP = 16 * Z
LAG_E, LAG_H = 6, 4


def iota(shape, dim):
    return lax.broadcasted_iota(I32, shape, dim)


class Copies:
    def __init__(self, sems):
        self.sems, self.used, self.open = sems, 0, []

    def start(self, source, target):
        copy = pltpu.make_async_copy(source, target, self.sems.at[self.used])
        self.used += 1
        copy.start()
        self.open.append(copy)

    def group(self):
        group, self.open = self.open, []
        return group

    def wait(self, group=None):
        for copy in self.group() if group is None else group:
            copy.wait()


def port_means(mean, cells):
    pick_y = (iota((Y, SLOTS), 0) == cells % Y).astype(F32)
    columns = jnp.dot(mean, pick_y, precision=HIGH, preferred_element_type=F32)
    return jnp.sum(jnp.where(iota((X, SLOTS), 0) == cells // Y, columns, 0.0), axis=0, keepdims=True)


def drawn_lanes(output_ref, state):
    lane, model = iota((MODELS, Y), 1), iota((MODELS, Y), 0)
    row = jnp.zeros((1, Y), F32)
    for q in range(2):
        drawn = jnp.sum(output_ref[:, q, :] * state, axis=1, keepdims=True)
        row = row + jnp.sum(
            jnp.where(lane == LANE_O + 2 * model + q, drawn, 0.0), axis=0, keepdims=True
        )
    return row


def pack_rows(read, up_ref, down_ref, c):
    low = iota((8, Y), 0) < 4
    for z in range(Z // 2):
        a, b = read(z), read(z + Z // 2)
        up_ref[16 * c + z] = jnp.where(low, a[:8], pltpu.roll(b[:8], 4, 0))
        down_ref[16 * c + z] = jnp.where(low, pltpu.roll(b[8:], 4, 0), a[8:])


def load_parts(copies, e_hbm, h_hbm, loss_hbm, gain_hbm, parts):
    sources = [e_hbm.at[c] for c in range(3)] + [h_hbm.at[c] for c in range(3)] + [loss_hbm, gain_hbm]
    groups = []
    for c, source in enumerate(sources):
        copies.start(source, parts.at[c])
        groups.append(copies.group())
    return groups


def first_kernel(
    e_hbm, h_hbm, loss_hbm, gain_hbm, feed_hbm, cells_hbm, state_hbm, output_hbm,
    even_out, odd_out, row_out, fixed_out,
    parts, feed, cells, state, output, sent, line, row, fixed, sems,
):
    copies = Copies(sems)
    groups = load_parts(copies, e_hbm, h_hbm, loss_hbm, gain_hbm, parts)
    for origin, target in ((feed_hbm, feed), (cells_hbm, cells), (state_hbm, state), (output_hbm, output)):
        copies.start(origin, target)
    small = copies.group()
    odd = lax.axis_index("fx") % 2
    for c in range(8):
        copies.wait(groups[c])
        pack_rows(lambda z: parts[c, z], sent.at[1 - odd], sent.at[odd], c)
        own = pl.ds(16 * c, 16)
        copies.start(sent.at[0, own], even_out.at[own])
        copies.start(sent.at[1, own], odd_out.at[own])
    copies.wait(small)
    mean = parts[2, 0]
    for z in range(1, Z):
        mean = mean + parts[2, z]
    line[...] = jnp.zeros_like(line)
    line[0:1, :SLOTS] = cells[...].astype(F32)
    for k in range(4):
        line[k + 1 : k + 2, :MODELS] = feed[k // 2, k % 2 : k % 2 + 1, :]
    lines = line[...]
    total = pltpu.roll(lines, LANE_C, 1)[0:1]
    for k in range(4):
        total = total + pltpu.roll(lines, LANE_D + 8 * k, 1)[k + 1 : k + 2]
    fixed[...] = total
    row[...] = jnp.broadcast_to(total + drawn_lanes(output, state[...]), row.shape)
    row[:, :SLOTS] = jnp.broadcast_to(port_means(mean * (1.0 / Z), cells[...]), (256, SLOTS))
    copies.start(row, row_out)
    copies.start(fixed, fixed_out)
    copies.wait()


def side_kernel(
    e_hbm, h_hbm, loss_hbm, gain_hbm, even_hbm, odd_hbm, halo_out, pack_out, even_out, odd_out,
    parts, got, halo, pack, sent, sems,
):
    copies = Copies(sems)
    groups = []
    sources = [e_hbm.at[c] for c in range(3)] + [h_hbm.at[c] for c in range(3)] + [loss_hbm, gain_hbm]
    for c, source in enumerate(sources):
        own = pl.ds(16 * c, 16)
        copies.start(even_hbm.at[own], got.at[0, own])
        copies.start(odd_hbm.at[own], got.at[1, own])
        copies.start(source, parts.at[c])
        groups.append(copies.group())
    odd = lax.axis_index("fx") % 2
    after, before = got.at[odd], got.at[1 - odd]
    odd = lax.axis_index(("fy", "grp")) % 2
    to_right, to_left = sent.at[odd], sent.at[1 - odd]
    low = iota((8, Y), 0) < 4
    group = iota((8, Y), 1) // 16
    half = iota((8, Y), 1) % 16 < 8
    for c in range(8):
        copies.wait(groups[c])
        for z in range(Z // 2):
            a, b = after[16 * c + z], before[16 * c + z]
            halo[c, z] = jnp.where(low, a, b)
            halo[c, z + Z // 2] = pltpu.roll(jnp.where(low, b, a), 4, 0)
        totals = []
        for part in range(4):
            total = [jnp.zeros((8, Y), F32)] * 3
            for zl in range(8):
                z = part * 8 + zl
                plane = parts[c, z]
                for i, tile in enumerate((plane[:8], plane[8:], halo[c, z])):
                    moved = pltpu.roll(tile, (16 * zl + 8) % Y, 1)
                    total[i] = jnp.where(group == zl, moved, total[i])
            totals.append(total)
            for i in range(3):
                pack[c, 8 * i : 8 * i + 8, Y * part : Y * part + Y] = total[i]
        for pair in range(2):
            for i in range(3):
                a, b = totals[2 * pair][i], totals[2 * pair + 1][i]
                rows, lanes = slice(8 * i, 8 * i + 8), slice(Y * pair, Y * pair + Y)
                to_right[c, rows, lanes] = jnp.where(half, a, pltpu.roll(b, 8, 1))
                to_left[c, rows, lanes] = jnp.where(half, pltpu.roll(a, Y - 8, 1), b)
        copies.start(pack.at[c], pack_out.at[c])
        copies.start(sent.at[0, c], even_out.at[c])
        copies.start(sent.at[1, c], odd_out.at[c])
        copies.start(halo.at[c], halo_out.at[c])
    copies.wait()


def index_kernel(
    counts_hbm, perm_hbm, gathered_hbm, moved_hbm, inputs_hbm, output_hbm, fixed_hbm,
    pick_out, mask_out, source_out, state_out, line_out,
    counts_ref, perm_ref, gathered, moved, inputs, output, fixed, pick, mask, source, new_state, line, sems,
):
    copies = Copies(sems)
    copies.start(counts_hbm, counts_ref)
    copies.start(perm_hbm, perm_ref)
    early = copies.group()
    pairs = ((gathered_hbm, gathered), (moved_hbm, moved), (inputs_hbm, inputs), (output_hbm, output), (fixed_hbm, fixed))
    for origin, target in pairs:
        copies.start(origin, target)
    late = copies.group()
    copies.wait(early)
    me, fx, fy = lax.axis_index(ALL), lax.axis_index("fx"), lax.axis_index(("fy", "grp"))
    counts = counts_ref[...]
    starts = counts
    for width in (1, 2, 4, 8, 16, 32, 64, 128):
        starts = starts + jnp.where(iota((1, 256), 1) >= width, pltpu.roll(starts, width, 1), 0)
    starts = starts - counts
    number = iota((LIST, 1), 0)
    slot = number % SLOTS
    dx, dy = number // SLOTS // 3 - 1, number // SLOTS % 3 - 1
    inside = (fx + dx >= 0) & (fx + dx < 8) & (fy + dy >= 0) & (fy + dy < 32)
    tile = jnp.where(inside, me + 32 * dx + dy, -1)
    own = iota((LIST, 256), 1) == tile
    start = jnp.sum(jnp.where(own, starts, 0), axis=1, keepdims=True)
    count = jnp.sum(jnp.where(own, counts, 0), axis=1, keepdims=True)
    live = slot < count
    wanted = jnp.where(live, start + slot, -1)
    even = iota((32, Y), 1) % 2 == 0
    perm = perm_ref[...]
    mates = jnp.where(even, pltpu.roll(perm, Y - 1, 1), pltpu.roll(perm, 1, 1))
    position = jnp.zeros((LIST, Y), I32)
    partner = jnp.zeros((LIST, Y), I32)
    spot = iota((2 * MODELS, Y), 0)
    mine_at = me * 2 * MODELS + 2 * (spot % MODELS) + spot // MODELS
    mine = jnp.zeros((2 * MODELS, Y), I32)
    for r in range(32):
        row, mate = perm[r : r + 1], mates[r : r + 1]
        hit = row == wanted
        position = jnp.where(hit, iota((LIST, Y), 1) + Y * r, position)
        partner = jnp.where(hit, mate, partner)
        mine = jnp.where(iota((2 * MODELS, Y), 1) + Y * r == mine_at, row, mine)
    position = jnp.sum(position, axis=1, keepdims=True)
    partner = jnp.sum(partner, axis=1, keepdims=True)
    mine = jnp.sum(mine, axis=1, keepdims=True)
    ports = jnp.concatenate([partner, mine], axis=0)
    total = LIST + 2 * MODELS
    before = starts <= ports
    port_tile = jnp.sum(before.astype(I32), axis=1, keepdims=True) - 1
    port_start = jnp.max(jnp.where(before, starts, 0), axis=1, keepdims=True)
    port_slot = ports - port_start
    pick[:LIST] = own.astype(F32).astype(jnp.bfloat16)
    pick[LIST : LIST + total] = (iota((total, 256), 1) == port_tile).astype(F32).astype(jnp.bfloat16)
    pick[LIST + total :] = (iota((LIST, 256), 1) == position // 16).astype(F32).astype(jnp.bfloat16)
    lane = iota((LIST, Y), 1)
    q = position % 2
    model = position // 2 % MODELS
    on = live.astype(F32)
    mask[OWN:MATE] = jnp.where(lane == slot, on, 0.0)
    mask[MATE:DRAWN] = (iota((total, Y), 1) == port_slot).astype(F32)
    mask[DRAWN:SELF] = jnp.where(lane == LANE_O + 2 * model + q, on, 0.0)
    mask[SELF:CROSS] = jnp.where(lane == LANE_D + 24 * q + model, on, 0.0)
    mask[CROSS:CELL] = jnp.where(lane == LANE_D + 8 * (q + 1) + model, on, 0.0)
    mask[CELL:] = (lane == LANE_C + slot).astype(F32)
    copies.start(pick, pick_out)
    copies.start(mask, mask_out)
    copies.wait(late)
    source[...], mine = port_sources(gathered, pick, mask)
    new_state[...] = moved[...] + input_part(inputs, mine)
    line[...] = fixed[...] + drawn_lanes(output, new_state[...])
    copies.start(source, source_out)
    copies.start(new_state, state_out)
    copies.start(line, line_out)
    copies.wait()


def port_sources(gathered_ref, pick_ref, mask_ref):
    gathered = gathered_ref[...]
    high = gathered.astype(jnp.bfloat16)
    left_over = gathered - high.astype(F32)
    middle = left_over.astype(jnp.bfloat16)
    low = (left_over - middle.astype(F32)).astype(jnp.bfloat16)
    picked = jnp.dot(
        pick_ref[...], jnp.concatenate([high, middle, low], axis=1), preferred_element_type=F32
    )
    picked = picked[:, :Y] + picked[:, Y : 2 * Y] + picked[:, 2 * Y :]
    total = LIST + 2 * MODELS

    def choose(part, mask):
        return jnp.sum(part * mask, axis=1, keepdims=True)

    of_tile, of_port, of_model = picked[:LIST], picked[LIST : LIST + total], picked[LIST + total :]
    own = choose(of_tile, mask_ref[OWN:MATE])
    others = choose(of_port, mask_ref[MATE:DRAWN])
    mate, mine = others[:LIST], others[LIST:]
    current = choose(
        of_model, mask_ref[DRAWN:SELF] + mask_ref[SELF:CROSS] * own + mask_ref[CROSS:CELL] * mate
    )
    cell = choose(of_tile, mask_ref[CELL:]).astype(I32)
    number = iota((LIST, 1), 0) // SLOTS
    x = (number // 3 - 1) * X + cell // Y
    y = (number % 3 - 1) * Y + cell % Y
    lane = iota((LIST, 2 * Y), 1)
    lane_y = jnp.where(lane < Y, lane, jnp.where(lane < Y + 16, lane - 136, jnp.where(lane < Y + 32, lane - 24, -1000)))
    row = iota((LIST, Y), 1)
    row_x = jnp.where(row < 20, row, jnp.where(row < 24, row - 24, -1000))
    spread = jnp.where(lane_y == y, current, 0.0)
    to_row = (row_x == x).astype(F32)
    source = lax.dot_general(
        to_row, spread, (((0,), (0,)), ((), ())), precision=HIGH, preferred_element_type=F32
    )[:24]
    return source, mine


def input_part(inputs, mine):
    return inputs[:, 0, :] * mine[:MODELS] + inputs[:, 1, :] * mine[MODELS:]


def repeat_groups(row_lanes):
    value = jnp.where(iota(row_lanes.shape, 1) < 16, row_lanes, 0.0)
    for width in (16, 32, 64):
        value = value + pltpu.roll(value, width, 1)
    return jnp.concatenate([value] * 4, axis=1)


def strip_step(fields, loss, gain, drive, keep_x, z_first, z_last):
    ex, ey, ez, hx, hy, hz = fields

    def up(v):
        return jnp.where(z_last, 0.0, pltpu.roll(v, STRIP - 16, 1))

    def down(v):
        return jnp.where(z_first, 0.0, pltpu.roll(v, 16, 1))

    hx = hx - COURANT * ((pltpu.roll(ez, STRIP - 1, 1) - ez) - (up(ey) - ey))
    hy = (hy - COURANT * ((up(ex) - ex) - (pltpu.roll(ez, 23, 0) - ez))) * keep_x
    hz = (hz - COURANT * ((pltpu.roll(ey, 23, 0) - ey) - (pltpu.roll(ex, STRIP - 1, 1) - ex))) * keep_x
    ex = loss * ex + gain * ((hz - pltpu.roll(hz, 1, 1)) - (hy - down(hy)))
    ey = loss * ey + gain * ((hx - down(hx)) - (hz - pltpu.roll(hz, 1, 0)))
    ez = loss * ez + gain * ((hy - pltpu.roll(hy, 1, 0)) - (hx - pltpu.roll(hx, 1, 1)) - drive)
    return [ex, ey, ez, hx, hy, hz]


def walls():
    keep_x = jnp.where((iota((24, 1), 0) >= 20) & (lax.axis_index("fx") == 0), 0.0, 1.0)
    return keep_x, jnp.where(lax.axis_index(("fy", "grp")) == 0, 0.0, 1.0)


def drives_of(source):
    return repeat_groups(source[:, Y:]), repeat_groups(pltpu.roll(source[:, Y:], Y - 16, 1))


def strips_step(s, strips, edge_coefs, seam, drives):
    keep_x, keep_y = walls()
    lanes = iota((24, STRIP), 1)
    ends = (keep_x, lanes < 16, lanes >= STRIP - 16)
    low_next = strip_step([strips[c] for c in range(6)], edge_coefs[0], edge_coefs[1], drives[0], *ends)
    for i, (e_at, h_at) in enumerate(((2, 3), (0, 5))):
        joined = jnp.where(lanes % 16 == 8, strips[6 + e_at], pltpu.roll(low_next[h_at] * keep_y, 2, 1))
        for part in range(4):
            seam[s, i, part] = joined[:, Y * part : Y * part + Y]
    high_next = strip_step([strips[6 + c] for c in range(6)], edge_coefs[2], edge_coefs[3], drives[1], *ends)
    for c in range(6):
        strips[c] = low_next[c]
        strips[6 + c] = high_next[c]


def sweep(s, state, coef, seam, source):
    keep_x, _ = walls()
    lane = iota((24, Y), 1)
    end, begin = lane == Y - 1, lane == 0

    def turned(z):
        turn = (247 - 16 * (z % 8)) % Y
        return pltpu.roll(seam[s, 0, z // 8], turn, 1), pltpu.roll(seam[s, 1, z // 8], turn, 1)

    def shift_electric(z):
        seam_a, seam_b = turned(z)
        return (
            jnp.where(end, seam_a, pltpu.roll(state[2, z], Y - 1, 1)),
            jnp.where(end, seam_b, pltpu.roll(state[0, z], Y - 1, 1)),
            seam_a,
            seam_b,
        )

    def magnetic(z, ez_next, ex_next, seam_a, seam_b):
        ex, ey, ez = state[0, z], state[1, z], state[2, z]
        hx = state[3, z + 1] - COURANT * ((ez_next - ez) - (state[1, z + 1] - ey))
        hy = state[4, z + 1] - COURANT * ((state[0, z + 1] - ex) - (pltpu.roll(ez, 23, 0) - ez))
        hz = state[5, z + 1] - COURANT * ((pltpu.roll(ey, 23, 0) - ey) - (ex_next - ex))
        hy = hy * keep_x
        hz = hz * keep_x
        state[3, z + 1] = hx
        state[4, z + 1] = hy
        state[5, z + 1] = hz
        return (
            jnp.where(begin, seam_a, pltpu.roll(hx, 1, 1)),
            jnp.where(begin, seam_b, pltpu.roll(hz, 1, 1)),
        )

    def electric(z, hx_before, hz_before):
        hx, hy, hz = state[3, z + 1], state[4, z + 1], state[5, z + 1]
        loss, gain = coef[0, z], coef[1, z]
        state[0, z] = loss * state[0, z] + gain * ((hz - hz_before) - (hy - state[4, z]))
        state[1, z] = loss * state[1, z] + gain * (
            (hx - state[3, z]) - (hz - pltpu.roll(hz, 1, 0))
        )
        state[2, z] = loss * state[2, z] + gain * (
            (hy - pltpu.roll(hy, 1, 0)) - (hx - hx_before) - source
        )

    shifted, magnetics = {}, {}
    for t in range(Z + LAG_E + LAG_H):
        if t < Z:
            shifted[t] = shift_electric(t)
        if 0 <= t - LAG_E < Z:
            magnetics[t - LAG_E] = magnetic(t - LAG_E, *shifted.pop(t - LAG_E))
        if 0 <= t - LAG_E - LAG_H:
            electric(t - LAG_E - LAG_H, *magnetics.pop(t - LAG_E - LAG_H))


def steps(first, state, coef, seam, strips, edge_coefs, source, begin, strips_done):
    drives = drives_of(source)
    strips_step(first, strips, edge_coefs, seam, drives)
    begin()
    for s in range(first, K):
        if s + 1 < K:
            strips_step(s + 1, strips, edge_coefs, seam, drives)
        else:
            strips_done()
        sweep(s, state, coef, seam, source[:, :Y])


def load_fields(copies, e_hbm, h_hbm, loss_hbm, gain_hbm, halo_hbm, state, coef):
    for c in range(3):
        copies.start(e_hbm.at[c], state.at[c, pl.ds(0, Z), pl.ds(0, X)])
        copies.start(h_hbm.at[c], state.at[3 + c, pl.ds(1, Z), pl.ds(0, X)])
    copies.start(loss_hbm, coef.at[0, :, pl.ds(0, X)])
    copies.start(gain_hbm, coef.at[1, :, pl.ds(0, X)])
    for i in range(2):
        copies.start(halo_hbm.at[6 + i], coef.at[i, :, pl.ds(X, 8)])
    for c in range(3):
        state[c, Z] = jnp.zeros((24, Y), F32)
        state[3 + c, 0] = jnp.zeros((24, Y), F32)


def store_fields(copies, state, e_out, h_out):
    for c in range(3):
        copies.start(state.at[c, pl.ds(0, Z), pl.ds(0, X)], e_out.at[c])
        copies.start(state.at[3 + c, pl.ds(1, Z), pl.ds(0, X)], h_out.at[c])


def first_block(
    e_hbm, h_hbm, loss_hbm, gain_hbm, halo_hbm, source_hbm, cells_hbm, line_hbm, pack_hbm, even_hbm, odd_hbm,
    e_out, h_out, row_out, even_out, odd_out, strips_out, edge_coefs_out,
    state, coef, seam, strips, edge_coefs, source, cells, line, pack, sent, got, row, sems,
):
    fx, fy = lax.axis_index("fx"), lax.axis_index(("fy", "grp"))
    right, left = got.at[fy % 2], got.at[1 - fy % 2]
    up, down = sent.at[1 - fx % 2], sent.at[fx % 2]
    copies = Copies(sems)
    pairs = ((source_hbm, source), (cells_hbm, cells), (line_hbm, line), (pack_hbm, pack), (even_hbm, got.at[0]), (odd_hbm, got.at[1]))
    for origin, target in pairs:
        copies.start(origin, target)
    edges = copies.group()
    load_fields(copies, e_hbm, h_hbm, loss_hbm, gain_hbm, halo_hbm, state, coef)
    for c in range(6):
        copies.start(halo_hbm.at[c], state.at[c, pl.ds(c // 3, Z), pl.ds(X, 8)])
    fields = copies.group()
    copies.wait(edges)
    half = iota((24, Y), 1) % 16 < 8
    for c in range(8):
        low_ref, high_ref = (strips.at[c], strips.at[6 + c]) if c < 6 else (edge_coefs.at[c - 6], edge_coefs.at[c - 4])
        for part in range(4):
            at, pair = slice(Y * part, Y * part + Y), slice(Y * (part // 2), Y * (part // 2) + Y)
            own, from_left, from_right = pack[c, :, at], left[c, :, pair], right[c, :, pair]
            if part % 2:
                from_left = pltpu.roll(from_left, Y - 8, 1)
            else:
                from_right = pltpu.roll(from_right, 8, 1)
            low_ref[:, at] = jnp.where(half, from_left, own)
            high_ref[:, at] = jnp.where(half, own, from_right)
    copies.start(edge_coefs, edge_coefs_out)

    def pack_strips():
        copies.start(strips.at[:, pl.ds(0, X)], strips_out)
        low = iota((8, Y), 0) < 4
        for i in range(12):
            for j in range(2):
                a, b = (strips[i, :X, Y * k : Y * k + Y] for k in (j, j + 2))
                up[96 + 2 * i + j] = jnp.where(low, a[:8], pltpu.roll(b[:8], 4, 0))
                down[96 + 2 * i + j] = jnp.where(low, pltpu.roll(b[8:], 4, 0), a[8:])

    steps(
        0, state, coef, seam, strips, edge_coefs, source[...], lambda: copies.wait(fields), pack_strips
    )
    store_fields(copies, state, e_out, h_out)
    for c in range(6):
        pack_rows(lambda z: state[c, z + c // 3, :X], up, down, c)
    copies.start(sent.at[0], even_out)
    copies.start(sent.at[1], odd_out)
    mean = state[2, 0, :X]
    for z in range(1, Z):
        mean = mean + state[2, z, :X]
    row[...] = jnp.broadcast_to(line[...], row.shape)
    row[:, :SLOTS] = jnp.broadcast_to(port_means(mean * (1.0 / Z), cells[...]), (256, SLOTS))
    copies.start(row, row_out)
    copies.wait()


def second_block_start(
    e_hbm, h_hbm, loss_hbm, gain_hbm, halo_hbm, strips_hbm, edge_coefs_hbm, even_hbm, odd_hbm,
    state_out, coef_out, strips_out, state, coef, seam, strips, edge_coefs, got, sems,
):
    fx = lax.axis_index("fx")
    after, before = got.at[fx % 2], got.at[1 - fx % 2]
    copies = Copies(sems)
    pairs = ((even_hbm, got.at[0]), (odd_hbm, got.at[1]), (strips_hbm, strips.at[:, pl.ds(0, X)]), (edge_coefs_hbm, edge_coefs))
    for origin, target in pairs:
        copies.start(origin, target)
    edges = copies.group()
    load_fields(copies, e_hbm, h_hbm, loss_hbm, gain_hbm, halo_hbm, state, coef)
    fields = copies.group()
    copies.wait(edges)
    low = iota((8, Y), 0) < 4
    for c in range(6):
        for z in range(Z // 2):
            a, b = after[16 * c + z], before[16 * c + z]
            state[c, z + c // 3, X:] = jnp.where(low, a, b)
            state[c, z + Z // 2 + c // 3, X:] = pltpu.roll(jnp.where(low, b, a), 4, 0)
    for i in range(12):
        for j in range(2):
            a, b = after[96 + 2 * i + j], before[96 + 2 * i + j]
            strips[i, X:, Y * j : Y * j + Y] = jnp.where(low, a, b)
            strips[i, X:, Y * (j + 2) : Y * (j + 3)] = pltpu.roll(jnp.where(low, b, a), 4, 0)
    none = jnp.zeros((24, STRIP), F32)
    strips_step(0, strips, edge_coefs, seam, (none, none))
    copies.start(strips, strips_out)
    copies.wait(fields)
    copies.start(coef, coef_out)
    sweep(0, state, coef, seam, jnp.zeros((24, Y), F32))
    copies.start(state, state_out)
    copies.wait()


def second_block_end(
    state_hbm, coef_hbm, strips_hbm, edge_coefs_hbm, pick_hbm, mask_hbm, moved_hbm, inputs_hbm, gathered_hbm,
    e_out, h_out, state_out,
    state, coef, seam, strips, edge_coefs, pick, mask, moved, inputs, gathered, result, sems,
):
    copies = Copies(sems)
    pairs = ((gathered_hbm, gathered), (pick_hbm, pick), (mask_hbm, mask), (moved_hbm, moved), (inputs_hbm, inputs))
    for origin, target in pairs:
        copies.start(origin, target)
    ready = copies.group()
    for origin, target in ((strips_hbm, strips), (edge_coefs_hbm, edge_coefs), (coef_hbm, coef), (state_hbm, state)):
        copies.start(origin, target)
    fields = copies.group()
    copies.wait(ready)
    source, mine = port_sources(gathered, pick, mask)
    result[...] = moved[...] + input_part(inputs, mine)
    copies.start(result, state_out)
    copies.wait(fields)
    for z in range(Z):
        state[2, z] = state[2, z] - coef[1, z] * source[:, :Y]
    for i, drive in enumerate(drives_of(source)):
        strips[6 * i + 2] = strips[6 * i + 2] - edge_coefs[2 * i + 1] * drive
    steps(1, state, coef, seam, strips, edge_coefs, source, lambda: None, lambda: None)
    store_fields(copies, state, e_out, h_out)
    copies.wait()


def shape(*dims, dtype=F32):
    return jax.ShapeDtypeStruct(dims, dtype)


def call(kernel, outs, scratch, cost=1_000_000):
    scratch = [pltpu.VMEM(dims, F32) if isinstance(dims, tuple) else dims for dims in scratch]
    place = pl.BlockSpec(memory_space=pl.ANY)

    def run(*args):
        return pl.pallas_call(
            kernel,
            out_shape=outs,
            in_specs=[place] * len(args),
            out_specs=jax.tree.map(lambda _: place, outs),
            scratch_shapes=scratch + [pltpu.SemaphoreType.DMA((64,))],
            compiler_params=pltpu.CompilerParams(vmem_limit_bytes=56 * 1024 * 1024),
            cost_estimate=pl.CostEstimate(flops=cost, bytes_accessed=cost, transcendentals=0),
        )(*args)

    return run


def gate(values, received, other):
    def nothing(*refs):
        pass

    place = pl.BlockSpec(memory_space=pl.ANY)
    return pl.pallas_call(
        nothing,
        out_shape=[shape(*value.shape) for value in values],
        in_specs=[place] * (len(values) + 2),
        out_specs=[place] * len(values),
        input_output_aliases={i: i for i in range(len(values))},
    )(*values, received, other)


def neighbours(even, odd, axes, count):
    later = [(i, i + 1) for i in range(1, count - 1, 2)]
    return (
        lax.ppermute(even, axes, [(i, i ^ 1) for i in range(count)]),
        lax.ppermute(odd, axes, later + [(j, i) for i, j in later]),
    )


def exchange(row):
    return lax.all_to_all(row, ALL, 0, 0, tiled=True)


def body(
    efield, hfield, loss, gain, port_count, port_perm, port_cell,
    pole_state, transition, input_map, output_map, feedthrough,
):
    inputs = jnp.swapaxes(input_map, 1, 2)
    feed = jnp.transpose(feedthrough, (1, 2, 0))
    ints = functools.partial(pltpu.VMEM, dtype=I32)
    picks = 2 * LIST + LIST + 2 * MODELS
    tiles8, tiles6 = (128, 8, Y), (120, 8, Y)

    even, odd, row, fixed = call(
        first_kernel,
        (shape(*tiles8), shape(*tiles8), shape(256, Y), shape(1, Y)),
        [(8, Z, X, Y), (2, 2, MODELS), ints((1, SLOTS)), (MODELS, 256), (MODELS, 2, 256)]
        + [(2,) + tiles8, (8, Y), (256, Y), (1, Y)],
    )(efield, hfield, loss, gain, feed, port_cell, pole_state, output_map)
    even, odd = neighbours(even, odd, "fx", 8)
    gathered = exchange(row)
    ends = (8, 24, STRIP // 2)
    halo, pack, even, odd = call(
        side_kernel,
        (shape(8, Z, 8, Y), shape(8, 24, STRIP), shape(*ends), shape(*ends)),
        [(8, Z, X, Y), (2,) + tiles8, (8, Z, 8, Y), (8, 24, STRIP), (2,) + ends],
    )(efield, hfield, loss, gain, even, odd)
    moved = jnp.einsum("mpr,mr->mp", transition, pole_state, precision=HIGH)
    even, odd = gate((even, odd), gathered, moved)
    even, odd = neighbours(even, odd, ("fy", "grp"), 32)
    bits = pltpu.VMEM((picks, 256), jnp.bfloat16)
    pick, mask, source, state, line = call(
        index_kernel,
        (shape(picks, 256, dtype=jnp.bfloat16), shape(MASKS, Y), shape(24, 256), shape(MODELS, 256), shape(1, Y)),
        [ints((1, 256)), ints((32, Y)), (256, Y), (MODELS, 256), (MODELS, 2, 256), (MODELS, 2, 256), (1, Y)]
        + [bits, (MASKS, Y), (24, 256), (MODELS, 256), (1, Y)],
    )(port_count.reshape(1, 256), port_perm.reshape(32, Y), gathered, moved, inputs, output_map, fixed)

    fields, coefs, edges = (6, Z + 1, 24, Y), (2, Z, 24, Y), (12, 24, STRIP)
    scratch = [fields, coefs, (K, 2, 4, 24, Y), edges, (4, 24, STRIP)]
    outs = (shape(3, Z, X, Y), shape(3, Z, X, Y))
    electric, magnetic, row, next_even, next_odd, strips, edge_coefs = call(
        first_block,
        outs
        + (shape(256, Y), shape(*tiles6), shape(*tiles6), shape(12, X, STRIP), shape(4, 24, STRIP)),
        scratch
        + [(24, 256), ints((1, SLOTS)), (1, Y), (8, 24, STRIP), (2,) + tiles6, (2,) + ends, (256, Y)],
    )(efield, hfield, loss, gain, halo, source, port_cell, line, pack, even, odd)

    even, odd = neighbours(next_even, next_odd, "fx", 8)
    gathered = exchange(row)
    moved = jnp.einsum("mpr,mr->mp", transition, state, precision=HIGH)
    begun, coef, strips = call(
        second_block_start,
        (shape(*fields), shape(*coefs), shape(*edges)),
        scratch + [(2,) + tiles6],
    )(electric, magnetic, loss, gain, halo, strips, edge_coefs, even, odd)
    return call(
        second_block_end,
        outs + (shape(MODELS, 256),),
        scratch + [bits, (MASKS, Y), (MODELS, 256), (MODELS, 2, 256), (256, Y), (MODELS, 256)],
    )(begun, coef, strips, edge_coefs, pick, mask, moved, inputs, gathered)


def solution(mesh):
    return jax.shard_map(
        body,
        mesh=mesh,
        in_specs=(
            P(None, None, "fx", ("fy", "grp")),
            P(None, None, "fx", ("fy", "grp")),
            P(None, "fx", ("fy", "grp")),
            P(None, "fx", ("fy", "grp")),
            P(),
            P(),
            P(ALL, None),
            P(ALL, None),
            P(ALL, None, None),
            P(ALL, None, None),
            P(ALL, None, None),
            P(ALL, None, None),
        ),
        out_specs=(
            P(None, None, "fx", ("fy", "grp")),
            P(None, None, "fx", ("fy", "grp")),
            P(ALL, None),
        ),
        check_vma=False,
    )
```

```python
import functools

import jax
import jax.numpy as jnp
from jax import lax
from jax.experimental import pallas as pl
from jax.experimental.pallas import tpu as pltpu
from jax.sharding import PartitionSpec as P

K = 4
BLOCKS = 2
COURANT = 0.5
HIGH = lax.Precision.HIGHEST
ALL = ("fx", "fy", "grp")
Z, X, Y = 32, 16, 128
SLOTS = 32
LIST = 9 * SLOTS
MODELS = 8
F32 = jnp.float32
I32 = jnp.int32
LANE_O, LANE_D, LANE_C = 32, 48, 80
OWN, MATE, DRAWN, SELF, CROSS, CELL, MASKS = 0, 288, 592, 880, 1168, 1456, 1744
STRIP = 16 * Z
LAG_E, LAG_H = 6, 4


def iota(shape, dim):
    return lax.broadcasted_iota(I32, shape, dim)


class Copies:
    def __init__(self, sems):
        self.sems, self.used, self.open = sems, 0, []

    def start(self, source, target):
        copy = pltpu.make_async_copy(source, target, self.sems.at[self.used])
        self.used += 1
        copy.start()
        self.open.append(copy)

    def group(self):
        group, self.open = self.open, []
        return group

    def wait(self, group=None):
        for copy in self.group() if group is None else group:
            copy.wait()


def port_means(mean, cells):
    pick_y = (iota((Y, SLOTS), 0) == cells % Y).astype(F32)
    columns = jnp.dot(mean, pick_y, precision=HIGH, preferred_element_type=F32)
    return jnp.sum(jnp.where(iota((X, SLOTS), 0) == cells // Y, columns, 0.0), axis=0, keepdims=True)


def drawn_lanes(output_ref, state):
    lane, model = iota((MODELS, Y), 1), iota((MODELS, Y), 0)
    row = jnp.zeros((1, Y), F32)
    for q in range(2):
        drawn = jnp.sum(output_ref[:, q, :] * state, axis=1, keepdims=True)
        row = row + jnp.sum(
            jnp.where(lane == LANE_O + 2 * model + q, drawn, 0.0), axis=0, keepdims=True
        )
    return row


def pack_rows(read, up_ref, down_ref, c):
    low = iota((8, Y), 0) < 4
    for z in range(Z // 2):
        a, b = read(z), read(z + Z // 2)
        up_ref[16 * c + z] = jnp.where(low, a[:8], pltpu.roll(b[:8], 4, 0))
        down_ref[16 * c + z] = jnp.where(low, pltpu.roll(b[8:], 4, 0), a[8:])


def load_parts(copies, e_hbm, h_hbm, loss_hbm, gain_hbm, parts):
    sources = [e_hbm.at[c] for c in range(3)] + [h_hbm.at[c] for c in range(3)] + [loss_hbm, gain_hbm]
    groups = []
    for c, source in enumerate(sources):
        copies.start(source, parts.at[c])
        groups.append(copies.group())
    return groups


def first_kernel(
    e_hbm, h_hbm, loss_hbm, gain_hbm, feed_hbm, cells_hbm, state_hbm, output_hbm,
    even_out, odd_out, row_out, fixed_out,
    parts, feed, cells, state, output, sent, line, row, fixed, sems,
):
    copies = Copies(sems)
    groups = load_parts(copies, e_hbm, h_hbm, loss_hbm, gain_hbm, parts)
    for origin, target in ((feed_hbm, feed), (cells_hbm, cells), (state_hbm, state), (output_hbm, output)):
        copies.start(origin, target)
    small = copies.group()
    odd = lax.axis_index("fx") % 2
    for c in range(8):
        copies.wait(groups[c])
        pack_rows(lambda z: parts[c, z], sent.at[1 - odd], sent.at[odd], c)
        own = pl.ds(16 * c, 16)
        copies.start(sent.at[0, own], even_out.at[own])
        copies.start(sent.at[1, own], odd_out.at[own])
    copies.wait(small)
    mean = parts[2, 0]
    for z in range(1, Z):
        mean = mean + parts[2, z]
    line[...] = jnp.zeros_like(line)
    line[0:1, :SLOTS] = cells[...].astype(F32)
    for k in range(4):
        line[k + 1 : k + 2, :MODELS] = feed[k // 2, k % 2 : k % 2 + 1, :]
    lines = line[...]
    total = pltpu.roll(lines, LANE_C, 1)[0:1]
    for k in range(4):
        total = total + pltpu.roll(lines, LANE_D + 8 * k, 1)[k + 1 : k + 2]
    fixed[...] = total
    row[...] = jnp.broadcast_to(total + drawn_lanes(output, state[...]), row.shape)
    row[:, :SLOTS] = jnp.broadcast_to(port_means(mean * (1.0 / Z), cells[...]), (256, SLOTS))
    copies.start(row, row_out)
    copies.start(fixed, fixed_out)
    copies.wait()


def side_kernel(
    e_hbm, h_hbm, loss_hbm, gain_hbm, even_hbm, odd_hbm, halo_out, pack_out, even_out, odd_out,
    parts, got, halo, pack, sent, sems,
):
    copies = Copies(sems)
    groups = []
    sources = [e_hbm.at[c] for c in range(3)] + [h_hbm.at[c] for c in range(3)] + [loss_hbm, gain_hbm]
    for c, source in enumerate(sources):
        own = pl.ds(16 * c, 16)
        copies.start(even_hbm.at[own], got.at[0, own])
        copies.start(odd_hbm.at[own], got.at[1, own])
        copies.start(source, parts.at[c])
        groups.append(copies.group())
    odd = lax.axis_index("fx") % 2
    after, before = got.at[odd], got.at[1 - odd]
    odd = lax.axis_index(("fy", "grp")) % 2
    to_right, to_left = sent.at[odd], sent.at[1 - odd]
    low = iota((8, Y), 0) < 4
    group = iota((8, Y), 1) // 16
    half = iota((8, Y), 1) % 16 < 8
    for c in range(8):
        copies.wait(groups[c])
        for z in range(Z // 2):
            a, b = after[16 * c + z], before[16 * c + z]
            halo[c, z] = jnp.where(low, a, b)
            halo[c, z + Z // 2] = pltpu.roll(jnp.where(low, b, a), 4, 0)
        totals = []
        for part in range(4):
            total = [jnp.zeros((8, Y), F32)] * 3
            for zl in range(8):
                z = part * 8 + zl
                plane = parts[c, z]
                for i, tile in enumerate((plane[:8], plane[8:], halo[c, z])):
                    moved = pltpu.roll(tile, (16 * zl + 8) % Y, 1)
                    total[i] = jnp.where(group == zl, moved, total[i])
            totals.append(total)
            for i in range(3):
                pack[c, 8 * i : 8 * i + 8, Y * part : Y * part + Y] = total[i]
        for pair in range(2):
            for i in range(3):
                a, b = totals[2 * pair][i], totals[2 * pair + 1][i]
                rows, lanes = slice(8 * i, 8 * i + 8), slice(Y * pair, Y * pair + Y)
                to_right[c, rows, lanes] = jnp.where(half, a, pltpu.roll(b, 8, 1))
                to_left[c, rows, lanes] = jnp.where(half, pltpu.roll(a, Y - 8, 1), b)
        copies.start(pack.at[c], pack_out.at[c])
        copies.start(sent.at[0, c], even_out.at[c])
        copies.start(sent.at[1, c], odd_out.at[c])
        copies.start(halo.at[c], halo_out.at[c])
    copies.wait()


def index_kernel(
    counts_hbm, perm_hbm, gathered_hbm, moved_hbm, inputs_hbm, output_hbm, fixed_hbm,
    pick_out, mask_out, source_out, state_out, line_out,
    counts_ref, perm_ref, gathered, moved, inputs, output, fixed, pick, mask, source, new_state, line, sems,
):
    copies = Copies(sems)
    copies.start(counts_hbm, counts_ref)
    copies.start(perm_hbm, perm_ref)
    early = copies.group()
    pairs = ((gathered_hbm, gathered), (moved_hbm, moved), (inputs_hbm, inputs), (output_hbm, output), (fixed_hbm, fixed))
    for origin, target in pairs:
        copies.start(origin, target)
    late = copies.group()
    copies.wait(early)
    me, fx, fy = lax.axis_index(ALL), lax.axis_index("fx"), lax.axis_index(("fy", "grp"))
    counts = counts_ref[...]
    starts = counts
    for width in (1, 2, 4, 8, 16, 32, 64, 128):
        starts = starts + jnp.where(iota((1, 256), 1) >= width, pltpu.roll(starts, width, 1), 0)
    starts = starts - counts
    number = iota((LIST, 1), 0)
    slot = number % SLOTS
    dx, dy = number // SLOTS // 3 - 1, number // SLOTS % 3 - 1
    inside = (fx + dx >= 0) & (fx + dx < 8) & (fy + dy >= 0) & (fy + dy < 32)
    tile = jnp.where(inside, me + 32 * dx + dy, -1)
    own = iota((LIST, 256), 1) == tile
    start = jnp.sum(jnp.where(own, starts, 0), axis=1, keepdims=True)
    count = jnp.sum(jnp.where(own, counts, 0), axis=1, keepdims=True)
    live = slot < count
    wanted = jnp.where(live, start + slot, -1)
    even = iota((32, Y), 1) % 2 == 0
    perm = perm_ref[...]
    mates = jnp.where(even, pltpu.roll(perm, Y - 1, 1), pltpu.roll(perm, 1, 1))
    position = jnp.zeros((LIST, Y), I32)
    partner = jnp.zeros((LIST, Y), I32)
    spot = iota((2 * MODELS, Y), 0)
    mine_at = me * 2 * MODELS + 2 * (spot % MODELS) + spot // MODELS
    mine = jnp.zeros((2 * MODELS, Y), I32)
    for r in range(32):
        row, mate = perm[r : r + 1], mates[r : r + 1]
        hit = row == wanted
        position = jnp.where(hit, iota((LIST, Y), 1) + Y * r, position)
        partner = jnp.where(hit, mate, partner)
        mine = jnp.where(iota((2 * MODELS, Y), 1) + Y * r == mine_at, row, mine)
    position = jnp.sum(position, axis=1, keepdims=True)
    partner = jnp.sum(partner, axis=1, keepdims=True)
    mine = jnp.sum(mine, axis=1, keepdims=True)
    ports = jnp.concatenate([partner, mine], axis=0)
    total = LIST + 2 * MODELS
    before = starts <= ports
    port_tile = jnp.sum(before.astype(I32), axis=1, keepdims=True) - 1
    port_start = jnp.max(jnp.where(before, starts, 0), axis=1, keepdims=True)
    port_slot = ports - port_start
    pick[:LIST] = own.astype(F32).astype(jnp.bfloat16)
    pick[LIST : LIST + total] = (iota((total, 256), 1) == port_tile).astype(F32).astype(jnp.bfloat16)
    pick[LIST + total :] = (iota((LIST, 256), 1) == position // 16).astype(F32).astype(jnp.bfloat16)
    lane = iota((LIST, Y), 1)
    q = position % 2
    model = position // 2 % MODELS
    on = live.astype(F32)
    mask[OWN:MATE] = jnp.where(lane == slot, on, 0.0)
    mask[MATE:DRAWN] = (iota((total, Y), 1) == port_slot).astype(F32)
    mask[DRAWN:SELF] = jnp.where(lane == LANE_O + 2 * model + q, on, 0.0)
    mask[SELF:CROSS] = jnp.where(lane == LANE_D + 24 * q + model, on, 0.0)
    mask[CROSS:CELL] = jnp.where(lane == LANE_D + 8 * (q + 1) + model, on, 0.0)
    mask[CELL:] = (lane == LANE_C + slot).astype(F32)
    copies.start(pick, pick_out)
    copies.start(mask, mask_out)
    copies.wait(late)
    source[...], mine = port_sources(gathered, pick, mask)
    new_state[...] = moved[...] + input_part(inputs, mine)
    line[...] = fixed[...] + drawn_lanes(output, new_state[...])
    copies.start(source, source_out)
    copies.start(new_state, state_out)
    copies.start(line, line_out)
    copies.wait()


def port_sources(gathered_ref, pick_ref, mask_ref):
    gathered = gathered_ref[...]
    high = gathered.astype(jnp.bfloat16)
    left_over = gathered - high.astype(F32)
    middle = left_over.astype(jnp.bfloat16)
    low = (left_over - middle.astype(F32)).astype(jnp.bfloat16)
    picked = jnp.dot(
        pick_ref[...], jnp.concatenate([high, middle, low], axis=1), preferred_element_type=F32
    )
    picked = picked[:, :Y] + picked[:, Y : 2 * Y] + picked[:, 2 * Y :]
    total = LIST + 2 * MODELS

    def choose(part, mask):
        return jnp.sum(part * mask, axis=1, keepdims=True)

    of_tile, of_port, of_model = picked[:LIST], picked[LIST : LIST + total], picked[LIST + total :]
    own = choose(of_tile, mask_ref[OWN:MATE])
    others = choose(of_port, mask_ref[MATE:DRAWN])
    mate, mine = others[:LIST], others[LIST:]
    current = choose(
        of_model, mask_ref[DRAWN:SELF] + mask_ref[SELF:CROSS] * own + mask_ref[CROSS:CELL] * mate
    )
    cell = choose(of_tile, mask_ref[CELL:]).astype(I32)
    number = iota((LIST, 1), 0) // SLOTS
    x = (number // 3 - 1) * X + cell // Y
    y = (number % 3 - 1) * Y + cell % Y
    lane = iota((LIST, 2 * Y), 1)
    lane_y = jnp.where(lane < Y, lane, jnp.where(lane < Y + 16, lane - 136, jnp.where(lane < Y + 32, lane - 24, -1000)))
    row = iota((LIST, Y), 1)
    row_x = jnp.where(row < 20, row, jnp.where(row < 24, row - 24, -1000))
    spread = jnp.where(lane_y == y, current, 0.0)
    to_row = (row_x == x).astype(F32)
    source = lax.dot_general(
        to_row, spread, (((0,), (0,)), ((), ())), precision=HIGH, preferred_element_type=F32
    )[:24]
    return source, mine


def input_part(inputs, mine):
    return inputs[:, 0, :] * mine[:MODELS] + inputs[:, 1, :] * mine[MODELS:]


def repeat_groups(row_lanes):
    value = jnp.where(iota(row_lanes.shape, 1) < 16, row_lanes, 0.0)
    for width in (16, 32, 64):
        value = value + pltpu.roll(value, width, 1)
    return jnp.concatenate([value] * 4, axis=1)


def strip_step(fields, loss, gain, drive, keep_x, z_first, z_last):
    ex, ey, ez, hx, hy, hz = fields

    def up(v):
        return jnp.where(z_last, 0.0, pltpu.roll(v, STRIP - 16, 1))

    def down(v):
        return jnp.where(z_first, 0.0, pltpu.roll(v, 16, 1))

    hx = hx - COURANT * ((pltpu.roll(ez, STRIP - 1, 1) - ez) - (up(ey) - ey))
    hy = (hy - COURANT * ((up(ex) - ex) - (pltpu.roll(ez, 23, 0) - ez))) * keep_x
    hz = (hz - COURANT * ((pltpu.roll(ey, 23, 0) - ey) - (pltpu.roll(ex, STRIP - 1, 1) - ex))) * keep_x
    ex = loss * ex + gain * ((hz - pltpu.roll(hz, 1, 1)) - (hy - down(hy)))
    ey = loss * ey + gain * ((hx - down(hx)) - (hz - pltpu.roll(hz, 1, 0)))
    ez = loss * ez + gain * ((hy - pltpu.roll(hy, 1, 0)) - (hx - pltpu.roll(hx, 1, 1)) - drive)
    return [ex, ey, ez, hx, hy, hz]


def walls():
    keep_x = jnp.where((iota((24, 1), 0) >= 20) & (lax.axis_index("fx") == 0), 0.0, 1.0)
    return keep_x, jnp.where(lax.axis_index(("fy", "grp")) == 0, 0.0, 1.0)


def drives_of(source):
    return repeat_groups(source[:, Y:]), repeat_groups(pltpu.roll(source[:, Y:], Y - 16, 1))


def strips_step(s, strips, edge_coefs, seam, drives):
    keep_x, keep_y = walls()
    lanes = iota((24, STRIP), 1)
    ends = (keep_x, lanes < 16, lanes >= STRIP - 16)
    low_next = strip_step([strips[c] for c in range(6)], edge_coefs[0], edge_coefs[1], drives[0], *ends)
    for i, (e_at, h_at) in enumerate(((2, 3), (0, 5))):
        joined = jnp.where(lanes % 16 == 8, strips[6 + e_at], pltpu.roll(low_next[h_at] * keep_y, 2, 1))
        for part in range(4):
            seam[s, i, part] = joined[:, Y * part : Y * part + Y]
    high_next = strip_step([strips[6 + c] for c in range(6)], edge_coefs[2], edge_coefs[3], drives[1], *ends)
    for c in range(6):
        strips[c] = low_next[c]
        strips[6 + c] = high_next[c]


def sweep(s, state, coef, seam, source):
    keep_x, _ = walls()
    lane = iota((24, Y), 1)
    end, begin = lane == Y - 1, lane == 0

    def turned(z):
        turn = (247 - 16 * (z % 8)) % Y
        return pltpu.roll(seam[s, 0, z // 8], turn, 1), pltpu.roll(seam[s, 1, z // 8], turn, 1)

    def shift_electric(z):
        seam_a, seam_b = turned(z)
        return (
            jnp.where(end, seam_a, pltpu.roll(state[2, z], Y - 1, 1)),
            jnp.where(end, seam_b, pltpu.roll(state[0, z], Y - 1, 1)),
            seam_a,
            seam_b,
        )

    def magnetic(z, ez_next, ex_next, seam_a, seam_b):
        ex, ey, ez = state[0, z], state[1, z], state[2, z]
        hx = state[3, z + 1] - COURANT * ((ez_next - ez) - (state[1, z + 1] - ey))
        hy = state[4, z + 1] - COURANT * ((state[0, z + 1] - ex) - (pltpu.roll(ez, 23, 0) - ez))
        hz = state[5, z + 1] - COURANT * ((pltpu.roll(ey, 23, 0) - ey) - (ex_next - ex))
        hy = hy * keep_x
        hz = hz * keep_x
        state[3, z + 1] = hx
        state[4, z + 1] = hy
        state[5, z + 1] = hz
        return (
            jnp.where(begin, seam_a, pltpu.roll(hx, 1, 1)),
            jnp.where(begin, seam_b, pltpu.roll(hz, 1, 1)),
        )

    def electric(z, hx_before, hz_before):
        hx, hy, hz = state[3, z + 1], state[4, z + 1], state[5, z + 1]
        loss, gain = coef[0, z], coef[1, z]
        state[0, z] = loss * state[0, z] + gain * ((hz - hz_before) - (hy - state[4, z]))
        state[1, z] = loss * state[1, z] + gain * (
            (hx - state[3, z]) - (hz - pltpu.roll(hz, 1, 0))
        )
        state[2, z] = loss * state[2, z] + gain * (
            (hy - pltpu.roll(hy, 1, 0)) - (hx - hx_before) - source
        )

    shifted, magnetics = {}, {}
    for t in range(Z + LAG_E + LAG_H):
        if t < Z:
            shifted[t] = shift_electric(t)
        if 0 <= t - LAG_E < Z:
            magnetics[t - LAG_E] = magnetic(t - LAG_E, *shifted.pop(t - LAG_E))
        if 0 <= t - LAG_E - LAG_H:
            electric(t - LAG_E - LAG_H, *magnetics.pop(t - LAG_E - LAG_H))


def steps(first, state, coef, seam, strips, edge_coefs, source, begin, strips_done):
    drives = drives_of(source)
    strips_step(first, strips, edge_coefs, seam, drives)
    begin()
    for s in range(first, K):
        if s + 1 < K:
            strips_step(s + 1, strips, edge_coefs, seam, drives)
        else:
            strips_done()
        sweep(s, state, coef, seam, source[:, :Y])


def load_fields(copies, e_hbm, h_hbm, loss_hbm, gain_hbm, halo_hbm, state, coef):
    for c in range(3):
        copies.start(e_hbm.at[c], state.at[c, pl.ds(0, Z), pl.ds(0, X)])
        copies.start(h_hbm.at[c], state.at[3 + c, pl.ds(1, Z), pl.ds(0, X)])
    copies.start(loss_hbm, coef.at[0, :, pl.ds(0, X)])
    copies.start(gain_hbm, coef.at[1, :, pl.ds(0, X)])
    for i in range(2):
        copies.start(halo_hbm.at[6 + i], coef.at[i, :, pl.ds(X, 8)])
    for c in range(3):
        state[c, Z] = jnp.zeros((24, Y), F32)
        state[3 + c, 0] = jnp.zeros((24, Y), F32)


def store_fields(copies, state, e_out, h_out):
    for c in range(3):
        copies.start(state.at[c, pl.ds(0, Z), pl.ds(0, X)], e_out.at[c])
        copies.start(state.at[3 + c, pl.ds(1, Z), pl.ds(0, X)], h_out.at[c])


def first_block(
    e_hbm, h_hbm, loss_hbm, gain_hbm, halo_hbm, source_hbm, cells_hbm, line_hbm, pack_hbm, even_hbm, odd_hbm,
    e_out, h_out, row_out, even_out, odd_out, strips_out, edge_coefs_out,
    state, coef, seam, strips, edge_coefs, source, cells, line, pack, sent, got, row, sems,
):
    fx, fy = lax.axis_index("fx"), lax.axis_index(("fy", "grp"))
    right, left = got.at[fy % 2], got.at[1 - fy % 2]
    up, down = sent.at[1 - fx % 2], sent.at[fx % 2]
    copies = Copies(sems)
    pairs = ((source_hbm, source), (cells_hbm, cells), (line_hbm, line), (pack_hbm, pack), (even_hbm, got.at[0]), (odd_hbm, got.at[1]))
    for origin, target in pairs:
        copies.start(origin, target)
    edges = copies.group()
    load_fields(copies, e_hbm, h_hbm, loss_hbm, gain_hbm, halo_hbm, state, coef)
    for c in range(6):
        copies.start(halo_hbm.at[c], state.at[c, pl.ds(c // 3, Z), pl.ds(X, 8)])
    fields = copies.group()
    copies.wait(edges)
    half = iota((24, Y), 1) % 16 < 8
    for c in range(8):
        low_ref, high_ref = (strips.at[c], strips.at[6 + c]) if c < 6 else (edge_coefs.at[c - 6], edge_coefs.at[c - 4])
        for part in range(4):
            at, pair = slice(Y * part, Y * part + Y), slice(Y * (part // 2), Y * (part // 2) + Y)
            own, from_left, from_right = pack[c, :, at], left[c, :, pair], right[c, :, pair]
            if part % 2:
                from_left = pltpu.roll(from_left, Y - 8, 1)
            else:
                from_right = pltpu.roll(from_right, 8, 1)
            low_ref[:, at] = jnp.where(half, from_left, own)
            high_ref[:, at] = jnp.where(half, own, from_right)
    copies.start(edge_coefs, edge_coefs_out)

    def send(tiles):
        copies.start(sent.at[0, tiles], even_out.at[tiles])
        copies.start(sent.at[1, tiles], odd_out.at[tiles])

    def pack_strips():
        copies.start(strips.at[:, pl.ds(0, X)], strips_out)
        low = iota((8, Y), 0) < 4
        for i in range(12):
            for j in range(2):
                a, b = (strips[i, :X, Y * k : Y * k + Y] for k in (j, j + 2))
                up[96 + 2 * i + j] = jnp.where(low, a[:8], pltpu.roll(b[:8], 4, 0))
                down[96 + 2 * i + j] = jnp.where(low, pltpu.roll(b[8:], 4, 0), a[8:])
        send(pl.ds(96, 24))

    steps(
        0, state, coef, seam, strips, edge_coefs, source[...], lambda: copies.wait(fields), pack_strips
    )
    store_fields(copies, state, e_out, h_out)
    mean = state[2, 0, :X]
    for z in range(1, Z):
        mean = mean + state[2, z, :X]
    row[...] = jnp.broadcast_to(line[...], row.shape)
    row[:, :SLOTS] = jnp.broadcast_to(port_means(mean * (1.0 / Z), cells[...]), (256, SLOTS))
    copies.start(row, row_out)
    for c in range(6):
        pack_rows(lambda z: state[c, z + c // 3, :X], up, down, c)
        send(pl.ds(16 * c, 16))
    copies.wait()


def second_block_start(
    e_hbm, h_hbm, loss_hbm, gain_hbm, halo_hbm, strips_hbm, edge_coefs_hbm, even_hbm, odd_hbm,
    state_out, coef_out, strips_out, state, coef, seam, strips, edge_coefs, got, sems,
):
    fx = lax.axis_index("fx")
    after, before = got.at[fx % 2], got.at[1 - fx % 2]
    copies = Copies(sems)
    pairs = ((even_hbm, got.at[0]), (odd_hbm, got.at[1]), (strips_hbm, strips.at[:, pl.ds(0, X)]), (edge_coefs_hbm, edge_coefs))
    for origin, target in pairs:
        copies.start(origin, target)
    edges = copies.group()
    load_fields(copies, e_hbm, h_hbm, loss_hbm, gain_hbm, halo_hbm, state, coef)
    fields = copies.group()
    copies.wait(edges)
    low = iota((8, Y), 0) < 4
    for c in range(6):
        for z in range(Z // 2):
            a, b = after[16 * c + z], before[16 * c + z]
            state[c, z + c // 3, X:] = jnp.where(low, a, b)
            state[c, z + Z // 2 + c // 3, X:] = pltpu.roll(jnp.where(low, b, a), 4, 0)
    for i in range(12):
        for j in range(2):
            a, b = after[96 + 2 * i + j], before[96 + 2 * i + j]
            strips[i, X:, Y * j : Y * j + Y] = jnp.where(low, a, b)
            strips[i, X:, Y * (j + 2) : Y * (j + 3)] = pltpu.roll(jnp.where(low, b, a), 4, 0)
    none = jnp.zeros((24, STRIP), F32)
    strips_step(0, strips, edge_coefs, seam, (none, none))
    copies.start(strips, strips_out)
    copies.wait(fields)
    copies.start(coef, coef_out)
    sweep(0, state, coef, seam, jnp.zeros((24, Y), F32))
    copies.start(state, state_out)
    copies.wait()


def second_block_end(
    state_hbm, coef_hbm, strips_hbm, edge_coefs_hbm, pick_hbm, mask_hbm, moved_hbm, inputs_hbm, gathered_hbm,
    e_out, h_out, state_out,
    state, coef, seam, strips, edge_coefs, pick, mask, moved, inputs, gathered, result, sems,
):
    copies = Copies(sems)
    pairs = ((gathered_hbm, gathered), (pick_hbm, pick), (mask_hbm, mask), (moved_hbm, moved), (inputs_hbm, inputs))
    for origin, target in pairs:
        copies.start(origin, target)
    ready = copies.group()
    for origin, target in ((strips_hbm, strips), (edge_coefs_hbm, edge_coefs), (coef_hbm, coef), (state_hbm, state)):
        copies.start(origin, target)
    fields = copies.group()
    copies.wait(ready)
    source, mine = port_sources(gathered, pick, mask)
    result[...] = moved[...] + input_part(inputs, mine)
    copies.start(result, state_out)
    copies.wait(fields)
    for z in range(Z):
        state[2, z] = state[2, z] - coef[1, z] * source[:, :Y]
    for i, drive in enumerate(drives_of(source)):
        strips[6 * i + 2] = strips[6 * i + 2] - edge_coefs[2 * i + 1] * drive
    steps(1, state, coef, seam, strips, edge_coefs, source, lambda: None, lambda: None)
    store_fields(copies, state, e_out, h_out)
    copies.wait()


def shape(*dims, dtype=F32):
    return jax.ShapeDtypeStruct(dims, dtype)


def call(kernel, outs, scratch, cost=1_000_000):
    scratch = [pltpu.VMEM(dims, F32) if isinstance(dims, tuple) else dims for dims in scratch]
    place = pl.BlockSpec(memory_space=pl.ANY)

    def run(*args):
        return pl.pallas_call(
            kernel,
            out_shape=outs,
            in_specs=[place] * len(args),
            out_specs=jax.tree.map(lambda _: place, outs),
            scratch_shapes=scratch + [pltpu.SemaphoreType.DMA((64,))],
            compiler_params=pltpu.CompilerParams(vmem_limit_bytes=56 * 1024 * 1024),
            cost_estimate=pl.CostEstimate(flops=cost, bytes_accessed=cost, transcendentals=0),
        )(*args)

    return run


def gate(values, received, other):
    def nothing(*refs):
        pass

    place = pl.BlockSpec(memory_space=pl.ANY)
    return pl.pallas_call(
        nothing,
        out_shape=[shape(*value.shape) for value in values],
        in_specs=[place] * (len(values) + 2),
        out_specs=[place] * len(values),
        input_output_aliases={i: i for i in range(len(values))},
    )(*values, received, other)


def neighbours(even, odd, axes, count):
    later = [(i, i + 1) for i in range(1, count - 1, 2)]
    return (
        lax.ppermute(even, axes, [(i, i ^ 1) for i in range(count)]),
        lax.ppermute(odd, axes, later + [(j, i) for i, j in later]),
    )


def exchange(row):
    return lax.all_to_all(row, ALL, 0, 0, tiled=True)


def body(
    efield, hfield, loss, gain, port_count, port_perm, port_cell,
    pole_state, transition, input_map, output_map, feedthrough,
):
    inputs = jnp.swapaxes(input_map, 1, 2)
    feed = jnp.transpose(feedthrough, (1, 2, 0))
    ints = functools.partial(pltpu.VMEM, dtype=I32)
    picks = 2 * LIST + LIST + 2 * MODELS
    tiles8, tiles6 = (128, 8, Y), (120, 8, Y)

    even, odd, row, fixed = call(
        first_kernel,
        (shape(*tiles8), shape(*tiles8), shape(256, Y), shape(1, Y)),
        [(8, Z, X, Y), (2, 2, MODELS), ints((1, SLOTS)), (MODELS, 256), (MODELS, 2, 256)]
        + [(2,) + tiles8, (8, Y), (256, Y), (1, Y)],
    )(efield, hfield, loss, gain, feed, port_cell, pole_state, output_map)
    even, odd = neighbours(even, odd, "fx", 8)
    gathered = exchange(row)
    ends = (8, 24, STRIP // 2)
    halo, pack, even, odd = call(
        side_kernel,
        (shape(8, Z, 8, Y), shape(8, 24, STRIP), shape(*ends), shape(*ends)),
        [(8, Z, X, Y), (2,) + tiles8, (8, Z, 8, Y), (8, 24, STRIP), (2,) + ends],
    )(efield, hfield, loss, gain, even, odd)
    moved = jnp.einsum("mpr,mr->mp", transition, pole_state, precision=HIGH)
    even, odd = gate((even, odd), gathered, moved)
    even, odd = neighbours(even, odd, ("fy", "grp"), 32)
    bits = pltpu.VMEM((picks, 256), jnp.bfloat16)
    pick, mask, source, state, line = call(
        index_kernel,
        (shape(picks, 256, dtype=jnp.bfloat16), shape(MASKS, Y), shape(24, 256), shape(MODELS, 256), shape(1, Y)),
        [ints((1, 256)), ints((32, Y)), (256, Y), (MODELS, 256), (MODELS, 2, 256), (MODELS, 2, 256), (1, Y)]
        + [bits, (MASKS, Y), (24, 256), (MODELS, 256), (1, Y)],
    )(port_count.reshape(1, 256), port_perm.reshape(32, Y), gathered, moved, inputs, output_map, fixed)

    fields, coefs, edges = (6, Z + 1, 24, Y), (2, Z, 24, Y), (12, 24, STRIP)
    scratch = [fields, coefs, (K, 2, 4, 24, Y), edges, (4, 24, STRIP)]
    outs = (shape(3, Z, X, Y), shape(3, Z, X, Y))
    electric, magnetic, row, next_even, next_odd, strips, edge_coefs = call(
        first_block,
        outs
        + (shape(256, Y), shape(*tiles6), shape(*tiles6), shape(12, X, STRIP), shape(4, 24, STRIP)),
        scratch
        + [(24, 256), ints((1, SLOTS)), (1, Y), (8, 24, STRIP), (2,) + tiles6, (2,) + ends, (256, Y)],
    )(efield, hfield, loss, gain, halo, source, port_cell, line, pack, even, odd)

    even, odd = neighbours(next_even, next_odd, "fx", 8)
    gathered = exchange(row)
    moved = jnp.einsum("mpr,mr->mp", transition, state, precision=HIGH)
    begun, coef, strips = call(
        second_block_start,
        (shape(*fields), shape(*coefs), shape(*edges)),
        scratch + [(2,) + tiles6],
    )(electric, magnetic, loss, gain, halo, strips, edge_coefs, even, odd)
    return call(
        second_block_end,
        outs + (shape(MODELS, 256),),
        scratch + [bits, (MASKS, Y), (MODELS, 256), (MODELS, 2, 256), (256, Y), (MODELS, 256)],
    )(begun, coef, strips, edge_coefs, pick, mask, moved, inputs, gathered)


def solution(mesh):
    return jax.shard_map(
        body,
        mesh=mesh,
        in_specs=(
            P(None, None, "fx", ("fy", "grp")),
            P(None, None, "fx", ("fy", "grp")),
            P(None, "fx", ("fy", "grp")),
            P(None, "fx", ("fy", "grp")),
            P(),
            P(),
            P(ALL, None),
            P(ALL, None),
            P(ALL, None, None),
            P(ALL, None, None),
            P(ALL, None, None),
            P(ALL, None, None),
        ),
        out_specs=(
            P(None, None, "fx", ("fy", "grp")),
            P(None, None, "fx", ("fy", "grp")),
            P(ALL, None),
        ),
        check_vma=False,
    )
```
